128 devices in a mesh: occ: 8 (over y, core), vir: 16 (over z, x).
Axes of the slice: x: 4, y: 4, z: 4, core: 2. Of those that a mesh axis runs over, the one named last changes fastest.
Arguments:
- amplitude: bfloat16 [16, 640, 8, 640], P(None, 'vir'), may hold values from -6 to 6
- integral: bfloat16 [8, 640, 16, 640], P(None, 'vir', 'occ'), may hold values from -0.25 to 0.25
- occ_irrep: int32 [16], replicated, may hold values from 0 to 7
- kocc_irrep: int32 [8], replicated, may hold values from 0 to 7
- vir_irrep: int32 [640], replicated, may hold values from 0 to 7, as said below
Outputs:
- residual: bfloat16 [16, 640, 16, 640], P(None, 'vir', 'occ')
The draws below stay inside these ranges and needn't reach their ends.
Inputs may be any that keep to these rules, and one draw needn't show every extreme that they name: `occ_irrep`: D2h irrep labels. `kocc_irrep`: D2h irrep labels. D2h irrep labels, ordered by irrep: vir_irrep never falls along the virtuals. The eight irreps hold, in an order that differs from draw to draw, 160, 120, three times 2 * 40 and three times 640 // 16 virtuals, so at most 160 virtuals share one irrep, and one irrep holds exactly that many.
All inputs are finite; a program needn't handle non-finite values.
Results may differ from the reference program's by a relative error of at most 0.0051.
Values may be sent and summed in bfloat16 or wider, within the bound.
A program may use at most 128 MiB of HBM per device.

```python
import jax
import jax.numpy as jnp
from jax import lax

V = 640
IB = 16
KB = 8


def draw_vir_irrep(key, part):
    key = jax.random.fold_in(key, 11)
    label_order = jax.random.permutation(key, 8)
    shares_all = jnp.array([4, 3, 2, 2, 2, 1, 1, 1], dtype=jnp.int32) * (V // 16)
    irrep_counts = jnp.take(shares_all, label_order)
    block_ends = jnp.cumsum(irrep_counts).astype(jnp.int32)
    positions = jnp.arange(V, dtype=jnp.int32)
    passed = (positions[:, None] >= block_ends[None, :]).astype(jnp.int32)
    return jnp.sum(passed, axis=1).astype(jnp.int32)


def place_ends(drawn, rng, least, top_value):
    index_at = [jax.random.randint(jax.random.fold_in(rng, axis), (), 0, length) for axis, length in enumerate(drawn.shape)]
    longest = drawn.shape.index(max(drawn.shape))
    neighbour = index_at[:longest] + [(index_at[longest] + 1) % drawn.shape[longest]] + index_at[longest + 1:]
    return drawn.at[tuple(index_at)].set(least).at[tuple(neighbour)].set(top_value)


def levels(own_key, extent, shards, least, high):
    level, own = 1.0, jax.random.fold_in(own_key, 6)
    for axis_at, parts in shards:
        draws = jnp.exp(jax.random.uniform(jax.random.fold_in(own, axis_at), (parts,), jnp.float32, least / len(shards), high / len(shards)))
        level = level * jnp.repeat(draws, extent[axis_at] // parts).reshape([-1 if axis == axis_at else 1 for axis in range(len(extent))])
    return level


def centred(rng, extent, scale, most, cuts=(), kind=jnp.bfloat16):
    result = scale * jax.random.normal(rng, extent, jnp.float32)
    if cuts:
        result = result * levels(rng, extent, cuts, -0.22, 0.18)
    return jnp.clip(result, -most, most).astype(kind)


def setup_inputs(seed: int = 0) -> dict:
    streams_of = jax.random.split(jax.random.key(seed), 6)
    amplitude = centred(streams_of[0], (IB, V, KB, V), 1.0, 6.0, ((1, 16),))
    integral = centred(streams_of[1], (KB, V, IB, V), (KB * V // 8) ** -0.5, 0.25, ((1, 16), (2, 8)))
    occ_irrep = place_ends(jax.random.randint(streams_of[2], (IB,), 0, 8), jax.random.fold_in(streams_of[2], 1), 0, 7).astype(jnp.int32)
    kocc_irrep = place_ends(jax.random.randint(streams_of[3], (KB,), 0, 8), jax.random.fold_in(streams_of[3], 1), 0, 7).astype(jnp.int32)
    vir_irrep = draw_vir_irrep(jax.random.fold_in(streams_of[5], 71), 0)
    return dict(amplitude=amplitude, integral=integral, occ_irrep=occ_irrep, kocc_irrep=kocc_irrep, vir_irrep=vir_irrep)


def reference(amplitude, integral, occ_irrep, kocc_irrep, vir_irrep):
    left = jnp.bitwise_xor(occ_irrep[:, None], vir_irrep[None, :])
    right = jnp.bitwise_xor(kocc_irrep[:, None], vir_irrep[None, :])
    tmask = left[:, :, None, None] == right[None, None, :, :]
    tsym = jnp.where(tmask, amplitude, jnp.zeros_like(amplitude))
    wmask = right[:, :, None, None] == left[None, None, :, :]
    wsym = jnp.where(wmask, integral, jnp.zeros_like(integral))
    wflat = wsym.reshape(KB * V, IB * V)

    def one_row(rows):
        flat = rows.reshape(V, KB * V)
        return jnp.dot(flat, wflat, preferred_element_type=jnp.float32).astype(jnp.bfloat16).reshape(V, IB, V)

    cycle = lax.map(one_row, tsym)

    def one_out(index):
        own = lax.dynamic_index_in_dim(cycle, index, 0, keepdims=False)
        other = lax.dynamic_index_in_dim(cycle, index, 2, keepdims=False)
        other = jnp.transpose(other, (2, 0, 1))
        return (own.astype(jnp.float32) + other.astype(jnp.float32)).astype(jnp.bfloat16)

    return lax.map(one_out, jnp.arange(IB, dtype=jnp.int32))
```

```python
import jax
import jax.numpy as jnp
from jax import lax
from jax.sharding import PartitionSpec as P

WIN = 160


def shards(amplitude, integral, occ_irrep, kocc_irrep, vir_irrep):
    vir_pos = lax.axis_index("vir")
    occ_pos = lax.axis_index("occ")
    local_a = amplitude.shape[1]
    local_j = integral.shape[2]
    n_occ = lax.axis_size("occ")
    n_vir = lax.axis_size("vir")
    nv = vir_irrep.shape[0]
    own = lax.dynamic_slice_in_dim(vir_irrep, vir_pos * local_a, 1)[0]
    j_labels = lax.dynamic_slice_in_dim(occ_irrep, occ_pos * local_j, local_j)
    firsts = jnp.sum((vir_irrep[None, :] < jnp.arange(8)[:, None]).astype(jnp.int32), axis=1)
    firsts = jnp.minimum(firsts, nv - WIN)

    def select(labels):
        start = jnp.sum(
            jnp.where(labels[..., None] == jnp.arange(8), firsts, 0), axis=-1
        )
        b = jnp.arange(nv)[:, None]
        n = jnp.arange(WIN)[None, :]
        hit = (b == n + start[..., None, None]) & (vir_irrep[:, None] == labels[..., None, None])
        return hit.astype(jnp.bfloat16)

    wlab = kocc_irrep[:, None] ^ j_labels[None, :] ^ own
    packed = jnp.einsum(
        "kcjb,kjbn->kcjn", integral, select(wlab), preferred_element_type=jnp.float32
    ).astype(jnp.bfloat16)
    packed = packed.reshape(packed.shape[0], local_a, local_j * WIN)
    panels = lax.all_gather(packed, "vir", axis=1, tiled=True)
    left = occ_irrep ^ own
    right = kocc_irrep[:, None] ^ vir_irrep[None, :]
    tmask = left[:, None, None, None] == right[None, None, :, :]
    tsym = jnp.where(tmask, amplitude, jnp.zeros_like(amplitude))
    cyc = jnp.einsum("iakc,kcn->ian", tsym, panels, preferred_element_type=jnp.float32).astype(jnp.bfloat16)
    batch = cyc.shape[0]
    cyc = cyc.reshape(batch, local_a, local_j, WIN)
    clab = left[:, None] ^ j_labels[None, :]
    cycle = jnp.einsum(
        "iajn,ijbn->iajb", cyc, select(clab), preferred_element_type=jnp.float32
    ).astype(jnp.bfloat16)
    width = nv
    moved = cycle.reshape(n_occ, local_j, local_a, local_j, n_vir, local_a)
    moved = jnp.transpose(moved, (0, 4, 1, 2, 3, 5)).reshape(n_occ * n_vir * local_j, local_a, local_j, local_a)
    moved = lax.all_to_all(moved, ("occ", "vir"), split_axis=0, concat_axis=0, tiled=True)
    moved = moved.reshape(n_occ, n_vir, local_j, local_a, local_j, local_a)
    mirror = jnp.transpose(moved, (0, 4, 5, 2, 1, 3)).reshape(batch, local_a, local_j, width)
    return (cycle.astype(jnp.float32) + mirror.astype(jnp.float32)).astype(jnp.bfloat16)


def solution(mesh):
    in_specs = (P(None, "vir", None, None), P(None, "vir", "occ", None), P(), P(), P())
    out_specs = P(None, "vir", "occ", None)
    return jax.shard_map(shards, mesh=mesh, in_specs=in_specs, out_specs=out_specs, check_vma=False)
```

```python
import functools
import jax
import jax.numpy as jnp
from jax import lax
from jax.experimental import pallas as pl
from jax.experimental.pallas import tpu as pltpu
from jax.sharding import PartitionSpec as P

WIN = 160
MESH = pl.DeviceIdType.MESH
CUT = 48


def gather_product(amp_ref, pack_ref, occ_ref, kocc_ref, lab_ref, virs_ref, out_ref,
                   amp, panels, tk, wk, acc, amp_sem, own_sem, send_sem, recv_sem):
    me = lax.axis_index("vir")
    z, x = me // 4, lax.rem(me, 4)
    batch, la, nk, nv = amp.shape
    pairs = batch // 2

    def amp_copy(i):
        return pltpu.make_async_copy(amp_ref.at[pl.ds(2 * i, 2)], amp.at[pl.ds(2 * i, 2)], amp_sem.at[i])

    for i in range(pairs):
        amp_copy(i).start()

    def at(h, p, q):
        p, q = lax.rem(p + 8, 4), lax.rem(q + 8, 4)
        return q * 4 + p if h == 0 else p * 4 + q

    here = [(x, z), (z, x)]
    barrier = pltpu.get_barrier_semaphore()
    for dp, dq in ((1, 0), (-1, 0), (0, 1), (0, -1)):
        pl.semaphore_signal(barrier, inc=1, device_id={"vir": at(0, x + dp, z + dq)}, device_id_type=MESH)
    own = [pltpu.make_async_copy(pack_ref.at[h], panels.at[h, me], own_sem.at[h]) for h in range(2)]
    for c in own:
        c.start()
    pl.semaphore_wait(barrier, 4)

    copies = []

    def send(h, block, rows, step, slot):
        p, q = here[h]
        v = at(h, p + block[0], q + block[1])
        ref = panels.at[h, v, pl.ds(rows[0], rows[1] - rows[0])]
        if block == (0, 0):
            src = pack_ref.at[h, pl.ds(rows[0], rows[1] - rows[0])]
        else:
            src = ref
        c = pltpu.make_async_remote_copy(
            src_ref=src, dst_ref=ref, send_sem=send_sem.at[h, slot], recv_sem=recv_sem.at[h, slot],
            device_id={"vir": at(h, p + step[0], q + step[1])}, device_id_type=MESH)
        c.start()
        copies.append(c)

    def arrived(h, block, rows, slot):
        p, q = here[h]
        v = at(h, p + block[0], q + block[1])
        ref = panels.at[h, v, pl.ds(rows[0], rows[1] - rows[0])]
        pltpu.make_async_remote_copy(
            src_ref=ref, dst_ref=ref, send_sem=send_sem.at[h, slot], recv_sem=recv_sem.at[h, slot],
            device_id={"vir": me}, device_id_type=MESH).wait_recv()

    full, low, high = (0, 2 * la), (0, CUT), (CUT, 2 * la)

    def second(h, d):
        send(h, (d, 0), full, (0, 1), 4 + 4 * d)
        send(h, (d, 0), full, (0, -1), 5 + 4 * d)

    rows = la * nk
    r = lax.broadcasted_iota(jnp.int32, (rows, rows), 0)
    c = lax.broadcasted_iota(jnp.int32, (rows, rows), 1)
    perm = (c == lax.rem(r, la) * nk + r // la).astype(jnp.float32).astype(jnp.bfloat16)
    mylab = virs_ref[me * la]

    def prepare(i):
        amp_copy(i).wait()
        parts = []
        for s in range(2):
            flat = amp[2 * i + s].reshape(rows, nv)
            moved = jnp.dot(perm, flat, preferred_element_type=jnp.float32)
            left = occ_ref[2 * i + s] ^ mylab
            parts.append([
                jnp.where(lab_ref[...] == (left ^ kocc_ref[k]), moved[k * la:(k + 1) * la], 0.0)
                for k in range(nk)])
        for k in range(nk):
            tk[k, pl.ds(2 * la * i, 2 * la), :] = jnp.concatenate(
                [parts[0][k], parts[1][k]], axis=0).astype(jnp.bfloat16)

    for h in range(2):
        send(h, (0, 0), full, (1, 0), 0)
        send(h, (0, 0), full, (-1, 0), 1)
        second(h, 0)
    prepare(0)
    prepare(1)
    for h in range(2):
        arrived(h, (-1, 0), full, 0)
        send(h, (-1, 0), low, (1, 0), 2)
        second(h, 3)
        arrived(h, (1, 0), full, 1)
        send(h, (1, 0), high, (-1, 0), 3)
        second(h, 1)

    def relay(h, d):
        b = d if d < 2 else d - 4
        arrived(h, (b, -1), full, 4 + 4 * d)
        send(h, (b, -1), low, (0, 1), 6 + 4 * d)
        arrived(h, (b, 1), full, 5 + 4 * d)
        send(h, (b, 1), high, (0, -1), 7 + 4 * d)

    prepare(2)
    for h in range(2):
        relay(h, 0)
    prepare(3)
    for h in range(2):
        arrived(h, (-2, 0), low, 2)
        arrived(h, (-2, 0), high, 3)
        second(h, 2)
    prepare(4)
    for h in range(2):
        relay(h, 3)
    prepare(5)
    for h in range(2):
        relay(h, 1)
    prepare(6)
    prepare(7)
    for h in range(2):
        relay(h, 2)
    for h in range(2):
        for d in range(4):
            b = d if d < 2 else d - 4
            arrived(h, (b, 2), low, 6 + 4 * d)
            arrived(h, (b, 2), high, 7 + 4 * d)
    for c in own:
        c.wait()
    for h in range(2):
        for v in range(0, 16, 2):
            one = panels[h, v].astype(jnp.float32)
            two = panels[h, v + 1].astype(jnp.float32)
            for kp in range(2):
                wk[kp, pl.ds(v * la, 2 * la), :] = jnp.concatenate(
                    [one[kp * la:(kp + 1) * la], two[kp * la:(kp + 1) * la]], axis=0).astype(jnp.bfloat16)
        for kp in range(2):
            k = 4 * h + 2 * kp
            a = jnp.dot(tk[k], wk[kp, :, 0:384], preferred_element_type=jnp.float32)
            b = jnp.dot(tk[k + 1], wk[kp, :, 256:640], preferred_element_type=jnp.float32)
            if k == 0:
                acc[0] = a
                acc[1] = b
            else:
                acc[0] += a
                acc[1] += b
    out_ref[...] = (acc[0][:, 0:320] + acc[1][:, 64:384]).astype(jnp.bfloat16)
    for c in copies:
        c.wait_send()


def cycle_windows(amplitude, pack, occ_irrep, kocc_irrep, vir_irrep):
    batch, la, nk, nv = amplitude.shape
    return pl.pallas_call(
        gather_product,
        out_shape=jax.ShapeDtypeStruct((batch * la, 320), jnp.bfloat16),
        in_specs=[
            pl.BlockSpec(memory_space=pl.ANY),
            pl.BlockSpec(memory_space=pltpu.VMEM),
            pl.BlockSpec(memory_space=pltpu.SMEM),
            pl.BlockSpec(memory_space=pltpu.SMEM),
            pl.BlockSpec(memory_space=pltpu.VMEM),
            pl.BlockSpec(memory_space=pltpu.SMEM),
        ],
        out_specs=pl.BlockSpec(memory_space=pltpu.VMEM),
        scratch_shapes=[
            pltpu.VMEM((batch, la, nk, nv), jnp.bfloat16),
            pltpu.VMEM((2, 16, 2 * la, 640), jnp.bfloat16),
            pltpu.VMEM((nk, batch * la, nv), jnp.bfloat16),
            pltpu.VMEM((2, nv, 640), jnp.bfloat16),
            pltpu.VMEM((2, batch * la, 384), jnp.float32),
            pltpu.SemaphoreType.DMA((batch // 2,)),
            pltpu.SemaphoreType.DMA((2,)),
            pltpu.SemaphoreType.DMA((2, 20)),
            pltpu.SemaphoreType.DMA((2, 20)),
        ],
        compiler_params=pltpu.CompilerParams(
            collective_id=0, has_side_effects=True, vmem_limit_bytes=48 * 1024 * 1024),
        name="gather_product",
    )(amplitude, pack, occ_irrep, kocc_irrep, vir_irrep.reshape(1, -1), vir_irrep)


def shards(amplitude, integral, occ_irrep, kocc_irrep, vir_irrep):
    vir_pos = lax.axis_index("vir")
    occ_pos = lax.axis_index("occ")
    local_a = amplitude.shape[1]
    local_j = integral.shape[2]
    n_occ = lax.axis_size("occ")
    n_vir = lax.axis_size("vir")
    nv = vir_irrep.shape[0]
    own = lax.dynamic_slice_in_dim(vir_irrep, vir_pos * local_a, 1)[0]
    j_labels = lax.dynamic_slice_in_dim(occ_irrep, occ_pos * local_j, local_j)
    firsts = jnp.sum((vir_irrep[None, :] < jnp.arange(8)[:, None]).astype(jnp.int32), axis=1)
    firsts = jnp.minimum(firsts, nv - WIN)

    def select(labels):
        start = jnp.sum(
            jnp.where(labels[..., None] == jnp.arange(8), firsts, 0), axis=-1
        )
        b = jnp.arange(nv)[:, None]
        n = jnp.arange(WIN)[None, :]
        hit = (b == n + start[..., None, None]) & (vir_irrep[:, None] == labels[..., None, None])
        return hit.astype(jnp.bfloat16)

    wlab = kocc_irrep[:, None] ^ j_labels[None, :] ^ own
    packed = jnp.einsum(
        "kcjb,kjbn->kcjn", integral, select(wlab), preferred_element_type=jnp.float32
    ).astype(jnp.bfloat16)
    packed = jnp.transpose(packed.reshape(2, 2, 2, local_a, local_j * WIN), (0, 1, 3, 2, 4)).reshape(2, 2 * local_a, 640)
    cyc = cycle_windows(amplitude, packed, occ_irrep, kocc_irrep, vir_irrep)
    left = occ_irrep ^ own
    batch = amplitude.shape[0]
    cyc = cyc.reshape(batch, local_a, local_j, WIN)
    clab = left[:, None] ^ j_labels[None, :]
    cycle = jnp.einsum(
        "iajn,ijbn->iajb", cyc, select(clab), preferred_element_type=jnp.float32
    ).astype(jnp.bfloat16)
    width = nv
    moved = cycle.reshape(n_occ, local_j, local_a, local_j, n_vir, local_a)
    moved = jnp.transpose(moved, (0, 4, 1, 2, 3, 5)).reshape(n_occ * n_vir * local_j, local_a, local_j, local_a)
    moved = lax.all_to_all(moved, ("occ", "vir"), split_axis=0, concat_axis=0, tiled=True)
    moved = moved.reshape(n_occ, n_vir, local_j, local_a, local_j, local_a)
    mirror = jnp.transpose(moved, (0, 4, 5, 2, 1, 3)).reshape(batch, local_a, local_j, width)
    return (cycle.astype(jnp.float32) + mirror.astype(jnp.float32)).astype(jnp.bfloat16)


def solution(mesh):
    in_specs = (P(None, "vir", None, None), P(None, "vir", "occ", None), P(), P(), P())
    out_specs = P(None, "vir", "occ", None)
    return jax.shard_map(shards, mesh=mesh, in_specs=in_specs, out_specs=out_specs, check_vma=False)
```

```python
import functools
import jax
import jax.numpy as jnp
from jax import lax
from jax.experimental import pallas as pl
from jax.experimental.pallas import tpu as pltpu
from jax.sharding import PartitionSpec as P

WIN = 160
FEW = 6
MESH = pl.DeviceIdType.MESH
CUT = 48


def cycle_kernel(groups, amp_ref, pack_ref, occ_ref, kocc_ref, lab_ref, virs_ref,
                 order, place, begin, block_of, group_of, member_of, out_ref,
                 amp, panels, tk, wk, acc, cw, comb, far, near, nearf, turned, pack_out, pack_in,
                 amp_sem, own_sem, send_sem, recv_sem, far_send, far_recv, occ_send, occ_recv):
    me = lax.axis_index("vir")
    mine = lax.axis_index("occ")
    z, x = me // 4, lax.rem(me, 4)
    batch, la, nk, nv = amp.shape
    pairs = batch // 2

    def amp_copy(i):
        return pltpu.make_async_copy(amp_ref.at[pl.ds(2 * i, 2)], amp.at[pl.ds(2 * i, 2)], amp_sem.at[i])

    for i in range(pairs):
        amp_copy(i).start()

    def at(h, p, q):
        p, q = lax.rem(p + 8, 4), lax.rem(q + 8, 4)
        return q * 4 + p if h == 0 else p * 4 + q

    here = [(x, z), (z, x)]
    barrier = pltpu.get_barrier_semaphore()
    for off in range(1, 16):
        pl.semaphore_signal(barrier, inc=1, device_id={"vir": at(0, x + off % 4, z + off // 4)}, device_id_type=MESH)
    for off in range(1, 8):
        pl.semaphore_signal(barrier, inc=1, device_id={"occ": lax.rem(mine + off, 8)}, device_id_type=MESH)
    own = [pltpu.make_async_copy(pack_ref.at[h], panels.at[h, me], own_sem.at[h]) for h in range(2)]
    for c in own:
        c.start()

    pl.semaphore_wait(barrier, 22)

    copies = []

    def send(h, block, rows, step, slot):
        p, q = here[h]
        v = at(h, p + block[0], q + block[1])
        ref = panels.at[h, v, pl.ds(rows[0], rows[1] - rows[0])]
        if block == (0, 0):
            src = pack_ref.at[h, pl.ds(rows[0], rows[1] - rows[0])]
        else:
            src = ref
        c = pltpu.make_async_remote_copy(
            src_ref=src, dst_ref=ref, send_sem=send_sem.at[h, slot], recv_sem=recv_sem.at[h, slot],
            device_id={"vir": at(h, p + step[0], q + step[1])}, device_id_type=MESH)
        c.start()
        copies.append(c)

    def arrived(h, block, rows, slot):
        p, q = here[h]
        v = at(h, p + block[0], q + block[1])
        ref = panels.at[h, v, pl.ds(rows[0], rows[1] - rows[0])]
        pltpu.make_async_remote_copy(
            src_ref=ref, dst_ref=ref, send_sem=send_sem.at[h, slot], recv_sem=recv_sem.at[h, slot],
            device_id={"vir": me}, device_id_type=MESH).wait_recv()

    full, low, high = (0, 2 * la), (0, CUT), (CUT, 2 * la)

    def second(h, d):
        send(h, (d, 0), full, (0, 1), 4 + 4 * d)
        send(h, (d, 0), full, (0, -1), 5 + 4 * d)

    rows = la * nk
    r = lax.broadcasted_iota(jnp.int32, (rows, rows), 0)
    c = lax.broadcasted_iota(jnp.int32, (rows, rows), 1)
    perm = (c == lax.rem(r, la) * nk + r // la).astype(jnp.float32).astype(jnp.bfloat16)
    mylab = virs_ref[me * la]

    for i in range(pairs):
        amp_copy(i).wait()

    def prepare(i):
        parts = []
        for s in range(2):
            orb = order[2 * i + s]
            flat = amp[orb].reshape(rows, nv)
            moved = jnp.dot(perm, flat, preferred_element_type=jnp.float32)
            left = occ_ref[orb] ^ mylab
            parts.append([
                jnp.where(lab_ref[...] == (left ^ kocc_ref[k]), moved[k * la:(k + 1) * la], 0.0)
                for k in range(nk)])
        for k in range(nk):
            tk[k, pl.ds(2 * la * i, 2 * la), :] = jnp.concatenate(
                [parts[0][k], parts[1][k]], axis=0).astype(jnp.bfloat16)

    for h in range(2):
        send(h, (0, 0), full, (1, 0), 0)
        send(h, (0, 0), full, (-1, 0), 1)
        second(h, 0)
    prepare(0)
    prepare(1)
    for h in range(2):
        arrived(h, (-1, 0), full, 0)
        send(h, (-1, 0), low, (1, 0), 2)
        second(h, 3)
        arrived(h, (1, 0), full, 1)
        send(h, (1, 0), high, (-1, 0), 3)
        second(h, 1)

    def relay(h, d):
        b = d if d < 2 else d - 4
        arrived(h, (b, -1), full, 4 + 4 * d)
        send(h, (b, -1), low, (0, 1), 6 + 4 * d)
        arrived(h, (b, 1), full, 5 + 4 * d)
        send(h, (b, 1), high, (0, -1), 7 + 4 * d)

    prepare(2)
    for h in range(2):
        relay(h, 0)
    prepare(3)
    for h in range(2):
        arrived(h, (-2, 0), low, 2)
        arrived(h, (-2, 0), high, 3)
        second(h, 2)
    prepare(4)
    for h in range(2):
        relay(h, 3)
    prepare(5)
    for h in range(2):
        relay(h, 1)
    prepare(6)
    prepare(7)
    for h in range(2):
        relay(h, 2)
    for h in range(2):
        for d in range(4):
            b = d if d < 2 else d - 4
            arrived(h, (b, 2), low, 6 + 4 * d)
            arrived(h, (b, 2), high, 7 + 4 * d)
    for c in own:
        c.wait()
    for h in range(2):
        for v in range(0, 16, 2):
            one = panels[h, v].astype(jnp.float32)
            two = panels[h, v + 1].astype(jnp.float32)
            for kp in range(2):
                wk[kp, pl.ds(v * la, 2 * la), :] = jnp.concatenate(
                    [one[kp * la:(kp + 1) * la], two[kp * la:(kp + 1) * la]], axis=0).astype(jnp.bfloat16)
        for kp in range(2):
            k = 4 * h + 2 * kp
            a = jnp.dot(tk[k], wk[kp, :, 0:384], preferred_element_type=jnp.float32)
            b = jnp.dot(tk[k + 1], wk[kp, :, 256:640], preferred_element_type=jnp.float32)
            if k == 0:
                acc[0] = a
                acc[1] = b
            else:
                acc[0] += a
                acc[1] += b
    whole = acc[0] + pltpu.roll(acc[1], 320, 1)
    wide = lax.broadcasted_iota(jnp.int32, whole.shape, 1)
    flatw = jnp.where(wide < 2 * WIN, whole, 0.0).astype(jnp.bfloat16).astype(jnp.float32)
    cw[...] = flatw.reshape(batch, la, 384)
    jocc = [occ_ref[2 * mine + j] for j in range(2)]

    spot = lax.broadcasted_iota(jnp.int32, (batch * la, 128), 1)
    for j in range(2):
        for r in range(4):
            start = WIN * j + la * r
            tile = start // 128 * 128
            width = 128 if start + la <= tile + 128 else 256
            total = None
            for g in range(3):
                piece = flatw[g * la:, tile:tile + width]
                shift = (la * g - (start - tile)) % width
                if shift:
                    piece = pltpu.roll(piece, shift, 1)
                piece = piece[:, :128]
                if g:
                    piece = jnp.concatenate([piece, jnp.zeros((g * la, 128), jnp.float32)], axis=0)
                total = piece if g == 0 else jnp.where(spot >= g * la, piece, total)
            comb[4 * j + r] = total.reshape(batch, la, 128)

    def message(r, v):
        lab = virs_ref[v * la]
        parts = []
        for j in range(2):
            base = begin[jocc[j] ^ lab ^ mylab]
            for q in range(groups):
                parts.append(comb[4 * j + r, base + 3 * q])
        return jnp.concatenate(parts, axis=0).astype(jnp.bfloat16)

    def far_copy(off, v, source):
        return pltpu.make_async_remote_copy(
            src_ref=far.at[v], dst_ref=near.at[source], send_sem=far_send.at[off], recv_sem=far_recv.at[off],
            device_id={"vir": v}, device_id_type=MESH)

    offs = [10, 9, 11, 6, 14, 2, 8, 5, 7, 13, 15, 1, 3, 4, 12]
    for off in offs:
        v = at(0, x + off % 4, z + off // 4)
        far[v] = message(lax.rem(x + off % 4, 4), v)
        far_copy(off, v, me).start()
    near[me] = message(x, me)
    nearf[me] = near[me].astype(jnp.float32).reshape(2 * groups, la, 128)
    for off in reversed(offs):
        source = at(0, x - off % 4, z - off // 4)
        pltpu.make_async_remote_copy(
            src_ref=near.at[source], dst_ref=near.at[source], send_sem=far_send.at[off], recv_sem=far_recv.at[off],
            device_id={"vir": source}, device_id_type=MESH).wait_recv()
        nearf[source] = near[source].astype(jnp.float32).reshape(2 * groups, la, 128)

    def windows(o):
        both = []
        for j in range(2):
            wins = []
            for s in range(2):
                orb = 2 * o + s
                lab = occ_ref[orb]
                want = lab ^ mylab ^ jocc[j]
                row = groups * j + group_of[orb]
                stack = [nearf[block_of[4 * want + d], row] for d in range(4)]
                stack = jnp.concatenate(stack + [jnp.zeros((96, 128), jnp.float32)], axis=0).T
                for m in range(3):
                    turned[2 * j + s, m] = stack[m * la:(m + 1) * la]
                win = turned[2 * j + s, member_of[orb]]
                wins.append(jnp.concatenate([win, jnp.zeros((la, 128), jnp.float32)], axis=1))
            both.append(wins[0] + pltpu.roll(wins[1], WIN, 1))
        return jnp.concatenate(both, axis=0).astype(jnp.bfloat16)

    def occ_copy(off, o, source):
        return pltpu.make_async_remote_copy(
            src_ref=pack_out.at[o], dst_ref=pack_in.at[source], send_sem=occ_send.at[off], recv_sem=occ_recv.at[off],
            device_id={"occ": o}, device_id_type=MESH)

    order_occ = [4, 5, 3, 2, 6, 7, 1]
    for off in order_occ:
        o = lax.rem(mine + off, 8)
        pack_out[o] = windows(o)
        occ_copy(off, o, mine).start()
    pack_in[mine] = windows(mine)

    tile_no = lax.broadcasted_iota(jnp.int32, (la, 640), 1) // WIN
    even = lax.rem(tile_no, 2) == 0

    def finish(o):
        back = pack_in[o].astype(jnp.float32)
        for j2 in range(2):
            orb = 2 * o + j2
            own_rows = cw[place[orb]]
            both = own_rows + back[j2 * la:(j2 + 1) * la]
            both = jnp.concatenate([both, jnp.zeros((la, 256), jnp.float32)], axis=1)
            both = both + pltpu.roll(both, 2 * WIN, 1)
            turn = pltpu.roll(both, WIN, 1)
            for j in range(2):
                want = occ_ref[orb] ^ mylab ^ jocc[j]
                row = jnp.where(even, both, turn) if j == 0 else jnp.where(even, turn, both)
                out_ref[orb, j] = jnp.where(lab_ref[...] == want, row, 0.0).astype(jnp.bfloat16)

    finish(mine)
    for off in reversed(order_occ):
        source = lax.rem(mine + 8 - off, 8)
        pltpu.make_async_remote_copy(
            src_ref=pack_in.at[source], dst_ref=pack_in.at[source], send_sem=occ_send.at[off],
            recv_sem=occ_recv.at[off], device_id={"occ": source}, device_id_type=MESH).wait_recv()
        finish(source)
    for c in copies:
        c.wait_send()
    for off in offs:
        far_copy(off, at(0, x + off % 4, z + off // 4), me).wait_send()
    for off in order_occ:
        occ_copy(off, lax.rem(mine + off, 8), mine).wait_send()


def residual_rows(groups, collective, amplitude, pack, occ_irrep, kocc_irrep, vir_row, vir_irrep, *tables):
    batch, la, nk, nv = amplitude.shape
    rows = 2 * groups * la
    return pl.pallas_call(
        functools.partial(cycle_kernel, groups),
        out_shape=jax.ShapeDtypeStruct((batch, 2, la, nv), jnp.bfloat16),
        in_specs=[
            pl.BlockSpec(memory_space=pl.ANY),
            pl.BlockSpec(memory_space=pltpu.VMEM),
            pl.BlockSpec(memory_space=pltpu.SMEM),
            pl.BlockSpec(memory_space=pltpu.SMEM),
            pl.BlockSpec(memory_space=pltpu.VMEM),
            pl.BlockSpec(memory_space=pltpu.SMEM),
        ] + [pl.BlockSpec(memory_space=pltpu.SMEM)] * 6,
        out_specs=pl.BlockSpec(memory_space=pltpu.VMEM),
        scratch_shapes=[
            pltpu.VMEM((batch, la, nk, nv), jnp.bfloat16),
            pltpu.VMEM((2, 16, 2 * la, 640), jnp.bfloat16),
            pltpu.VMEM((nk, batch * la, nv), jnp.bfloat16),
            pltpu.VMEM((2, nv, 640), jnp.bfloat16),
            pltpu.VMEM((2, batch * la, 384), jnp.float32),
            pltpu.VMEM((batch, la, 384), jnp.float32),
            pltpu.VMEM((8, batch, la, 128), jnp.float32),
            pltpu.VMEM((16, rows, 128), jnp.bfloat16),
            pltpu.VMEM((16, rows, 128), jnp.bfloat16),
            pltpu.VMEM((16, 2 * groups, la, 128), jnp.float32),
            pltpu.VMEM((4, 3, la, 256), jnp.float32),
            pltpu.VMEM((8, 2 * la, 384), jnp.bfloat16),
            pltpu.VMEM((8, 2 * la, 384), jnp.bfloat16),
            pltpu.SemaphoreType.DMA((batch // 2,)),
            pltpu.SemaphoreType.DMA((2,)),
            pltpu.SemaphoreType.DMA((2, 20)),
            pltpu.SemaphoreType.DMA((2, 20)),
            pltpu.SemaphoreType.DMA((16,)),
            pltpu.SemaphoreType.DMA((16,)),
            pltpu.SemaphoreType.DMA((8,)),
            pltpu.SemaphoreType.DMA((8,)),
        ],
        compiler_params=pltpu.CompilerParams(
            collective_id=collective, has_side_effects=True, vmem_limit_bytes=56 * 1024 * 1024),
        name="cycle_residual",
    )(amplitude, pack, occ_irrep, kocc_irrep, vir_row, vir_irrep, *tables)


def prepare_kernel(occ_ref, kocc_ref, lab_ref, virs_ref, w_ref, pack_ref, few_ref, *tables):
    nk, la = w_ref.shape[0], w_ref.shape[1]
    me = lax.axis_index("vir")
    mine = lax.axis_index("occ")
    mylab = virs_ref[me * la]
    quarter = lax.broadcasted_iota(jnp.int32, (la, 640), 1) // WIN
    for h in range(2):
        both = []
        for kp in range(2):
            total = None
            for k2 in range(2):
                k = 4 * h + 2 * kp + k2
                for j in range(2):
                    want = kocc_ref[k] ^ occ_ref[2 * mine + j] ^ mylab
                    part = jnp.where(lab_ref[...] == want, w_ref[k, :, j, :].astype(jnp.float32), 0.0)
                    part = part + pltpu.roll(part, 2 * WIN, 1)
                    part = part + pltpu.roll(part, WIN, 1)
                    total = part if total is None else jnp.where(quarter >= 2 * k2 + j, part, total)
            both.append(total)
        pack_ref[h] = jnp.concatenate(both, axis=0).astype(jnp.bfloat16)

    batch = occ_ref.shape[0]
    occ = [occ_ref[i] for i in range(batch)]
    blocks = [virs_ref[la * v] for v in range(16)]

    def count(terms):
        total = jnp.int32(0)
        for t in terms:
            total = total + t.astype(jnp.int32)
        return total

    places = [count([(occ[o] <= occ[i]) if o < i else (occ[o] < occ[i]) for o in range(batch) if o != i])
              for i in range(batch)]
    below = [count([occ[o] < r for o in range(batch)]) for r in range(8)] + [jnp.int32(batch)]
    most = jnp.int32(0)
    for r in range(8):
        most = jnp.maximum(most, below[r + 1] - below[r])
    few_ref[0] = most
    for t, groups in enumerate((2, 6)):
        order, place, begin, block_of, group_of, member_of = tables[6 * t:6 * t + 6]
        for r in range(8):
            begin[r] = jnp.minimum(below[r], max(batch - 3 * groups, 0))
            for d in range(4):
                p = jnp.int32(0)
                for q in range(4):
                    p = p + jnp.where(blocks[4 * q + d] == r, 4 * q + d, 0)
                block_of[4 * r + d] = p
        for i in range(batch):
            place[i] = places[i]
            slot = places[i] - begin[occ[i]]
            group = count([slot >= 3 * q for q in range(1, groups)])
            group_of[i] = group
            member_of[i] = slot - 3 * group
            order[places[i]] = i


def prepare(occ_irrep, kocc_irrep, vir_row, vir_irrep, integral):
    smem, vmem = pl.BlockSpec(memory_space=pltpu.SMEM), pl.BlockSpec(memory_space=pltpu.VMEM)
    sizes = (16, 16, 8, 32, 16, 16)
    found = pl.pallas_call(
        prepare_kernel,
        out_shape=[jax.ShapeDtypeStruct((2, 80, 640), jnp.bfloat16), jax.ShapeDtypeStruct((1,), jnp.int32)]
        + [jax.ShapeDtypeStruct((n,), jnp.int32) for n in sizes + sizes],
        in_specs=[smem, smem, vmem, smem, vmem],
        out_specs=[vmem] + [smem] * 13,
        name="prepare",
    )(occ_irrep, kocc_irrep, vir_row, vir_irrep, integral)
    return found[0], found[1], found[2:8], found[8:14]


def shards(amplitude, integral, occ_irrep, kocc_irrep, vir_irrep):
    vir_row = vir_irrep.reshape(1, -1)
    pack, most, few_tables, all_tables = prepare(occ_irrep, kocc_irrep, vir_row, vir_irrep, integral)
    args = (amplitude, pack, occ_irrep, kocc_irrep, vir_row, vir_irrep)
    rows = lax.cond(
        most[0] <= FEW,
        lambda *a: residual_rows(2, 0, *a, *few_tables),
        lambda *a: residual_rows(6, 1, *a, *all_tables),
        *args,
    )
    return jnp.transpose(rows, (0, 2, 1, 3))


def solution(mesh):
    in_specs = (P(None, "vir", None, None), P(None, "vir", "occ", None), P(), P(), P())
    out_specs = P(None, "vir", "occ", None)
    return jax.shard_map(shards, mesh=mesh, in_specs=in_specs, out_specs=out_specs, check_vma=False)
```

```python
import functools
import jax
import jax.numpy as jnp
from jax import lax
from jax.experimental import pallas as pl
from jax.experimental.pallas import tpu as pltpu
from jax.sharding import PartitionSpec as P

WIN = 160
FEW = 6
MESH = pl.DeviceIdType.MESH
CUT = 48
ORDER, PLACE, BEGIN, BLOCK, GROUP, MEMBER, MOST = 0, 16, 32, 40, 72, 88, 104


def table_kernel(groups, occ_ref, virs_ref, tab):
    batch = occ_ref.shape[0]
    la = virs_ref.shape[0] // 16
    occ = [occ_ref[i] for i in range(batch)]
    places = [jnp.int32(0)] * batch
    for i in range(batch):
        for o in range(i):
            before = (occ[o] <= occ[i]).astype(jnp.int32)
            places[i] = places[i] + before
            places[o] = places[o] + (1 - before)
    below = []
    for r in range(8):
        total = jnp.int32(0)
        for o in range(batch):
            total = total + (occ[o] < r).astype(jnp.int32)
        below.append(total)
    below.append(jnp.int32(batch))
    most = jnp.int32(0)
    for r in range(8):
        most = jnp.maximum(most, below[r + 1] - below[r])
        tab[BEGIN + r] = jnp.minimum(below[r], max(batch - 3 * groups, 0))
        for d in range(4):
            tab[BLOCK + 4 * r + d] = jnp.int32(0)
    for i in range(MOST, 128):
        tab[i] = most
    for v in range(16):
        tab[BLOCK + 4 * virs_ref[la * v] + v % 4] = jnp.int32(v)
    for i in range(batch):
        tab[PLACE + i] = places[i]
        tab[ORDER + places[i]] = jnp.int32(i)
        slot = places[i] - tab[BEGIN + occ[i]]
        group = jnp.int32(0)
        for q in range(1, groups):
            group = group + (slot >= 3 * q).astype(jnp.int32)
        tab[GROUP + i] = group
        tab[MEMBER + i] = slot - 3 * group


def make_table(groups, occ_irrep, vir_irrep):
    smem = pl.BlockSpec(memory_space=pltpu.SMEM)
    return pl.pallas_call(
        functools.partial(table_kernel, groups),
        out_shape=jax.ShapeDtypeStruct((128,), jnp.int32),
        in_specs=[smem, smem],
        out_specs=smem,
        name="make_table",
    )(occ_irrep, vir_irrep)


def cycle_kernel(groups, amp_ref, w_ref, occ_ref, kocc_ref, lab_ref, virs_ref, tab, out_ref,
                 amp, panels, tk, wk, acc, rowp, lanep, cw, comb, far, near, nearf, turned, pack_out, pack_in,
                 amp_sem, send_sem, recv_sem, far_send, far_recv, occ_send, occ_recv):
    me = lax.axis_index("vir")
    mine = lax.axis_index("occ")
    z, x = me // 4, lax.rem(me, 4)
    batch, la, nk, nv = amp.shape
    pairs = batch // 2
    here = [(x, z), (z, x)]

    amp_copies = [
        pltpu.make_async_copy(amp_ref.at[pl.ds(2 * i, 2)], amp.at[pl.ds(2 * i, 2)], amp_sem.at[i])
        for i in range(pairs)]
    for c in amp_copies:
        c.start()

    def at(h, p, q):
        p, q = lax.rem(p + 8, 4), lax.rem(q + 8, 4)
        return q * 4 + p if h == 0 else p * 4 + q

    barrier = pltpu.get_barrier_semaphore()
    for off in range(1, 16):
        pl.semaphore_signal(barrier, inc=1, device_id={"vir": at(0, x + off % 4, z + off // 4)}, device_id_type=MESH)
    for off in range(1, 8):
        pl.semaphore_signal(barrier, inc=1, device_id={"occ": lax.rem(mine + off, 8)}, device_id_type=MESH)

    labs = lab_ref[...].reshape(1, nv)
    mylab = virs_ref[me * la]
    jocc = [occ_ref[2 * mine + j] for j in range(2)]

    quarter = lax.broadcasted_iota(jnp.int32, (la, nv), 1) // WIN

    def pack(h):
        both = []
        for kp in range(2):
            total = None
            for k2 in range(2):
                k = 4 * h + 2 * kp + k2
                for j in range(2):
                    want = kocc_ref[k] ^ jocc[j] ^ mylab
                    part = jnp.where(labs == want, w_ref[k, :, j, :].astype(jnp.float32), 0.0)
                    part = part + pltpu.roll(part, 2 * WIN, 1)
                    part = part + pltpu.roll(part, WIN, 1)
                    total = part if total is None else jnp.where(quarter >= 2 * k2 + j, part, total)
            both.append(total)
        panels[h, me] = jnp.concatenate(both, axis=0).astype(jnp.bfloat16)

    copies = []

    def send(h, block, rows, step, slot):
        p, q = here[h]
        ref = panels.at[h, at(h, p + block[0], q + block[1]), pl.ds(rows[0], rows[1] - rows[0])]
        c = pltpu.make_async_remote_copy(
            src_ref=ref, dst_ref=ref, send_sem=send_sem.at[h, slot], recv_sem=recv_sem.at[h, slot],
            device_id={"vir": at(h, p + step[0], q + step[1])}, device_id_type=MESH)
        c.start()
        copies.append(c)

    def arrived(h, block, rows, slot):
        p, q = here[h]
        ref = panels.at[h, at(h, p + block[0], q + block[1]), pl.ds(rows[0], rows[1] - rows[0])]
        pltpu.make_async_remote_copy(
            src_ref=ref, dst_ref=ref, send_sem=send_sem.at[h, slot], recv_sem=recv_sem.at[h, slot],
            device_id={"vir": me}, device_id_type=MESH).wait_recv()

    full, low, high = (0, 2 * la), (0, CUT), (CUT, 2 * la)

    def second(h, d):
        send(h, (d, 0), full, (0, 1), 4 + 4 * d)
        send(h, (d, 0), full, (0, -1), 5 + 4 * d)

    def relay(h, d):
        b = d if d < 2 else d - 4
        arrived(h, (b, -1), full, 4 + 4 * d)
        send(h, (b, -1), low, (0, 1), 6 + 4 * d)
        arrived(h, (b, 1), full, 5 + 4 * d)
        send(h, (b, 1), high, (0, -1), 7 + 4 * d)

    def one_hot(n, source):
        r = lax.broadcasted_iota(jnp.int32, (n, n), 0)
        c = lax.broadcasted_iota(jnp.int32, (n, n), 1)
        return source(r, c).astype(jnp.float32).astype(jnp.bfloat16)

    rows = la * nk

    def prepare(i):
        parts = []
        for s in range(2):
            orb = tab[ORDER + 2 * i + s]
            moved = jnp.dot(rowp[...], amp[orb].reshape(rows, nv), preferred_element_type=jnp.float32)
            left = occ_ref[orb] ^ mylab
            parts.append([
                jnp.where(labs == (left ^ kocc_ref[k]), moved[k * la:(k + 1) * la], 0.0)
                for k in range(nk)])
        here_rows = pl.ds(2 * la * i, 2 * la)
        for k in range(nk // 2):
            tk[k, here_rows, :] = jnp.concatenate([parts[0][k], parts[1][k]], axis=0).astype(jnp.bfloat16)
        rest = jnp.concatenate([parts[s][k] for k in range(nk // 2, nk) for s in range(2)], axis=0)
        rest = jnp.dot(rest.astype(jnp.bfloat16), lanep[...], preferred_element_type=jnp.float32)
        for k in range(nk // 2, nk):
            at_row = 2 * la * (k - nk // 2)
            tk[k, here_rows, :] = rest[at_row:at_row + 2 * la].astype(jnp.bfloat16)

    def multiply(h, dq, first):
        q = lax.rem(here[h][1] + dq + 4, 4)
        blocks = [panels[h, at(h, p, q)].astype(jnp.float32) for p in range(4)]
        for kp in range(2):
            wk[h, q, pl.ds(pl.multiple_of(256 * kp + 32 * q, 32), WIN), :] = jnp.concatenate(
                [b[kp * la:(kp + 1) * la] for b in blocks], axis=0).astype(jnp.bfloat16)
        lanes = pl.ds(pl.multiple_of(128 * q, 128), 256)
        for k2 in range(2):
            t = jnp.concatenate([tk[4 * h + k2, :, lanes], tk[4 * h + 2 + k2, :, lanes]], axis=1)
            part = jnp.dot(t, wk[h, q, :, 256 * k2:256 * k2 + 384], preferred_element_type=jnp.float32)
            if first:
                acc[k2] = part
            else:
                acc[k2] += part

    pack(0)
    pl.semaphore_wait(barrier, 22)
    send(0, (0, 0), full, (1, 0), 0)
    send(0, (0, 0), full, (-1, 0), 1)
    second(0, 0)
    pack(1)
    send(1, (0, 0), full, (1, 0), 0)
    send(1, (0, 0), full, (-1, 0), 1)
    second(1, 0)
    rowp[...] = one_hot(rows, lambda r, c: c == lax.rem(r, la) * nk + r // la)
    lanep[...] = one_hot(
        nv, lambda r, c: r == (4 * (lax.rem(c, WIN) // la) + c // WIN) * la + lax.rem(c, la))
    for h in range(2):
        wk[h] = jnp.zeros(wk.shape[1:], wk.dtype)
    for c in amp_copies:
        c.wait()
    prepare(0)
    for h in range(2):
        arrived(h, (-1, 0), full, 0)
        send(h, (-1, 0), low, (1, 0), 2)
        second(h, 3)
        arrived(h, (1, 0), full, 1)
        send(h, (1, 0), high, (-1, 0), 3)
        second(h, 1)
    prepare(1)
    for h in range(2):
        relay(h, 0)
    prepare(2)
    for h in range(2):
        arrived(h, (-2, 0), low, 2)
        arrived(h, (-2, 0), high, 3)
        second(h, 2)
    prepare(3)
    prepare(4)
    for h in range(2):
        relay(h, 3)
    prepare(5)
    for h in range(2):
        relay(h, 1)
    prepare(6)
    prepare(7)
    multiply(0, 0, True)
    multiply(1, 0, False)
    for h in range(2):
        relay(h, 2)
    for h in range(2):
        multiply(h, -1, False)
        multiply(h, 1, False)
    for h in range(2):
        for d in range(4):
            b = d if d < 2 else d - 4
            arrived(h, (b, 2), low, 6 + 4 * d)
            arrived(h, (b, 2), high, 7 + 4 * d)
        multiply(h, 2, False)

    whole = acc[0] + pltpu.roll(acc[1], 2 * WIN, 1)
    wide = lax.broadcasted_iota(jnp.int32, whole.shape, 1)
    whole = jnp.where(wide < 2 * WIN, whole, 0.0).astype(jnp.bfloat16).astype(jnp.float32)
    cw[...] = whole.reshape(batch, la, 384)

    spot = lax.broadcasted_iota(jnp.int32, (batch * la, 128), 1)

    def combine(j):
        for r in range(4):
            start = WIN * j + la * r
            tile = start // 128 * 128
            width = 128 if start + la <= tile + 128 else 256
            total = None
            for g in range(3):
                piece = whole[g * la:, tile:tile + width]
                shift = (la * g - (start - tile)) % width
                if shift:
                    piece = pltpu.roll(piece, shift, 1)
                piece = piece[:, :128]
                if g:
                    piece = jnp.concatenate([piece, jnp.zeros((g * la, 128), jnp.float32)], axis=0)
                total = piece if g == 0 else jnp.where(spot >= g * la, piece, total)
            comb[4 * j + r] = total.reshape(batch, la, 128)

    def message(j, r, v):
        base = tab[BEGIN + (jocc[j] ^ virs_ref[v * la] ^ mylab)]
        parts = [comb[4 * j + r, base + 3 * q] for q in range(groups)]
        return jnp.concatenate(parts, axis=0).astype(jnp.bfloat16)

    def far_copy(j, off, v, source):
        return pltpu.make_async_remote_copy(
            src_ref=far.at[j, v], dst_ref=near.at[j, source], send_sem=far_send.at[j, off],
            recv_sem=far_recv.at[j, off], device_id={"vir": v}, device_id_type=MESH)

    offs = [10, 9, 11, 6, 14, 2, 8, 5, 7, 13, 15, 1, 3, 4, 12]
    for j in range(2):
        combine(j)
        for off in offs:
            v = at(0, x + off % 4, z + off // 4)
            far[j, v] = message(j, lax.rem(x + off % 4, 4), v)
            far_copy(j, off, v, me).start()

    def take(j, source, value):
        nearf[source, groups * j:groups * (j + 1)] = value.astype(jnp.float32).reshape(groups, la, 128)

    def windows(j, o):
        wins = []
        for s in range(2):
            orb = 2 * o + s
            want = occ_ref[orb] ^ mylab ^ jocc[j]
            row = groups * j + tab[GROUP + orb]
            stack = [nearf[tab[BLOCK + 4 * want + d], row] for d in range(4)]
            stack = jnp.concatenate(stack + [jnp.zeros((96, 128), jnp.float32)], axis=0).T
            for m in range(3):
                turned[s, m] = stack[m * la:(m + 1) * la]
            wins.append(turned[s, tab[MEMBER + orb]])
        rest = wins[0][:, 128:] + pltpu.roll(wins[1][:, 128:], 32, 1)
        return jnp.concatenate(
            [wins[0][:, :128], wins[1][:, :128], rest, jnp.zeros((8, 128), jnp.float32)], axis=0).astype(jnp.bfloat16)

    def occ_copy(j, off, o, source):
        return pltpu.make_async_remote_copy(
            src_ref=pack_out.at[j, o], dst_ref=pack_in.at[j, source], send_sem=occ_send.at[j, off],
            recv_sem=occ_recv.at[j, off], device_id={"occ": o}, device_id_type=MESH)

    order_occ = [4, 5, 3, 2, 6, 7, 1]
    for j in range(2):
        take(j, me, message(j, x, me))
        for off in reversed(offs):
            source = at(0, x - off % 4, z - off // 4)
            far_copy(j, off, source, source).wait_recv()
            take(j, source, near[j, source])
        for off in order_occ:
            o = lax.rem(mine + off, 8)
            pack_out[j, o] = windows(j, o)
            occ_copy(j, off, o, mine).start()
        pack_in[j, mine] = windows(j, mine)

    even = lax.rem(quarter, 2) == 0
    thin = lax.broadcasted_iota(jnp.int32, (la, 128), 1) < 32
    none = jnp.zeros((la, 128), jnp.float32)

    def finish(i2, o):
        orb = 2 * o + i2
        back = pack_in[i2, o].astype(jnp.float32)
        rest = back[2 * la:3 * la]
        one = jnp.concatenate([back[:la], jnp.where(thin, rest, 0.0), none, none, none], axis=1)
        two = jnp.concatenate([back[la:2 * la], jnp.where(thin, pltpu.roll(rest, 96, 1), 0.0), none, none, none], axis=1)
        both = jnp.concatenate([cw[tab[PLACE + orb]], none, none], axis=1) + one + pltpu.roll(two, WIN, 1)
        both = both + pltpu.roll(both, 2 * WIN, 1)
        turn = pltpu.roll(both, WIN, 1)
        for j in range(2):
            want = occ_ref[orb] ^ mylab ^ jocc[j]
            row = jnp.where(even, both, turn) if j == 0 else jnp.where(even, turn, both)
            out_ref[orb, j] = jnp.where(labs == want, row, 0.0).astype(jnp.bfloat16)

    for i2 in range(2):
        finish(i2, mine)
        for off in reversed(order_occ):
            source = lax.rem(mine + 8 - off, 8)
            occ_copy(i2, off, source, source).wait_recv()
            finish(i2, source)
    for c in copies:
        c.wait_send()
    for j in range(2):
        for off in offs:
            far_copy(j, off, at(0, x + off % 4, z + off // 4), me).wait_send()
        for off in order_occ:
            occ_copy(j, off, lax.rem(mine + off, 8), mine).wait_send()


def residual_rows(groups, collective, amplitude, integral, occ_irrep, kocc_irrep, vir_irrep, table):
    batch, la, nk, nv = amplitude.shape
    rows = groups * la
    smem, vmem = pl.BlockSpec(memory_space=pltpu.SMEM), pl.BlockSpec(memory_space=pltpu.VMEM)
    return pl.pallas_call(
        functools.partial(cycle_kernel, groups),
        out_shape=jax.ShapeDtypeStruct((batch, 2, la, nv), jnp.bfloat16),
        in_specs=[pl.BlockSpec(memory_space=pl.ANY), vmem, smem, smem, vmem, smem, smem],
        out_specs=vmem,
        scratch_shapes=[
            pltpu.VMEM((batch, la, nk, nv), jnp.bfloat16),
            pltpu.VMEM((2, 16, 2 * la, 640), jnp.bfloat16),
            pltpu.VMEM((nk, batch * la, nv), jnp.bfloat16),
            pltpu.VMEM((2, 4, 512, 640), jnp.bfloat16),
            pltpu.VMEM((2, batch * la, 384), jnp.float32),
            pltpu.VMEM((la * nk, la * nk), jnp.bfloat16),
            pltpu.VMEM((nv, nv), jnp.bfloat16),
            pltpu.VMEM((batch, la, 384), jnp.float32),
            pltpu.VMEM((8, batch, la, 128), jnp.float32),
            pltpu.VMEM((2, 16, rows, 128), jnp.bfloat16),
            pltpu.VMEM((2, 16, rows, 128), jnp.bfloat16),
            pltpu.VMEM((16, 2 * groups, la, 128), jnp.float32),
            pltpu.VMEM((2, 3, la, 256), jnp.float32),
            pltpu.VMEM((2, 8, 128, 128), jnp.bfloat16),
            pltpu.VMEM((2, 8, 128, 128), jnp.bfloat16),
            pltpu.SemaphoreType.DMA((batch // 2,)),
            pltpu.SemaphoreType.DMA((2, 20)),
            pltpu.SemaphoreType.DMA((2, 20)),
            pltpu.SemaphoreType.DMA((2, 16)),
            pltpu.SemaphoreType.DMA((2, 16)),
            pltpu.SemaphoreType.DMA((2, 8)),
            pltpu.SemaphoreType.DMA((2, 8)),
        ],
        compiler_params=pltpu.CompilerParams(
            collective_id=collective, has_side_effects=True, vmem_limit_bytes=56 * 1024 * 1024),
        name="cycle_residual",
    )(amplitude, integral, occ_irrep, kocc_irrep, vir_irrep, vir_irrep, table)


def shards(amplitude, integral, occ_irrep, kocc_irrep, vir_irrep):
    table = make_table(2, occ_irrep, vir_irrep)
    args = (amplitude, integral, occ_irrep, kocc_irrep, vir_irrep)
    rows = lax.cond(
        table[MOST] <= FEW,
        lambda *a: residual_rows(2, 0, *a, table),
        lambda *a: residual_rows(6, 1, *a, make_table(6, occ_irrep, vir_irrep)),
        *args,
    )
    return jnp.transpose(rows, (0, 2, 1, 3))


def solution(mesh):
    in_specs = (P(None, "vir", None, None), P(None, "vir", "occ", None), P(), P(), P())
    out_specs = P(None, "vir", "occ", None)
    return jax.shard_map(shards, mesh=mesh, in_specs=in_specs, out_specs=out_specs, check_vma=False)
```

```python
import functools
import jax
import jax.numpy as jnp
from jax import lax
from jax.experimental import pallas as pl
from jax.experimental.pallas import tpu as pltpu
from jax.sharding import PartitionSpec as P

WIN = 160
FEW = 6
MESH = pl.DeviceIdType.MESH
ORDER, PLACE, BEGIN, BLOCK, GROUP, MEMBER, MOST = 0, 16, 32, 40, 72, 88, 104


def table_kernel(groups, occ_ref, virs_ref, tab):
    batch = occ_ref.shape[0]
    la = virs_ref.shape[0] // 16
    occ = [occ_ref[i] for i in range(batch)]
    places = [jnp.int32(0)] * batch
    for i in range(batch):
        for o in range(i):
            before = (occ[o] <= occ[i]).astype(jnp.int32)
            places[i] = places[i] + before
            places[o] = places[o] + (1 - before)
    below = []
    for r in range(8):
        total = jnp.int32(0)
        for o in range(batch):
            total = total + (occ[o] < r).astype(jnp.int32)
        below.append(total)
    below.append(jnp.int32(batch))
    most = jnp.int32(0)
    for r in range(8):
        most = jnp.maximum(most, below[r + 1] - below[r])
        tab[BEGIN + r] = jnp.minimum(below[r], max(batch - 3 * groups, 0))
        for d in range(4):
            tab[BLOCK + 4 * r + d] = jnp.int32(0)
    for i in range(MOST, 128):
        tab[i] = most
    for v in range(16):
        tab[BLOCK + 4 * virs_ref[la * v] + v % 4] = jnp.int32(v)
    for i in range(batch):
        tab[PLACE + i] = places[i]
        tab[ORDER + places[i]] = jnp.int32(i)
        slot = places[i] - tab[BEGIN + occ[i]]
        group = jnp.int32(0)
        for q in range(1, groups):
            group = group + (slot >= 3 * q).astype(jnp.int32)
        tab[GROUP + i] = group
        tab[MEMBER + i] = slot - 3 * group


def make_table(groups, occ_irrep, vir_irrep):
    smem = pl.BlockSpec(memory_space=pltpu.SMEM)
    return pl.pallas_call(
        functools.partial(table_kernel, groups),
        out_shape=jax.ShapeDtypeStruct((128,), jnp.int32),
        in_specs=[smem, smem],
        out_specs=smem,
        name="make_table",
    )(occ_irrep, vir_irrep)


def cycle_kernel(groups, amp_ref, w_ref, occ_ref, kocc_ref, lab_ref, virs_ref, tab, out_ref,
                 amp, panels, tk, wk, acc, rowp, cw, comb, far, near, nearf, turned, pack_out, pack_in,
                 amp_sem, send_sem, recv_sem, far_send, far_recv, occ_send, occ_recv):
    me = lax.axis_index("vir")
    mine = lax.axis_index("occ")
    z, x = me // 4, lax.rem(me, 4)
    batch, la, nk, nv = amp.shape
    pairs = batch // 2
    here = [(x, z), (z, x)]

    amp_copies = [
        pltpu.make_async_copy(amp_ref.at[pl.ds(2 * i, 2)], amp.at[pl.ds(2 * i, 2)], amp_sem.at[i])
        for i in range(pairs)]
    for c in amp_copies:
        c.start()

    def at(h, p, q):
        p, q = lax.rem(p + 8, 4), lax.rem(q + 8, 4)
        return q * 4 + p if h == 0 else p * 4 + q

    def beside(off):
        return lax.rem(z + off // 4, 4) * 4 + lax.rem(x + lax.rem(off, 4), 4)

    def behind(off):
        return lax.rem(z + 4 - off // 4, 4) * 4 + lax.rem(x + 4 - lax.rem(off, 4), 4)

    barrier = pltpu.get_barrier_semaphore()

    @pl.loop(1, 16)
    def _(off):
        pl.semaphore_signal(barrier, inc=1, device_id={"vir": beside(off)}, device_id_type=MESH)

    @pl.loop(1, 8)
    def _(off):
        pl.semaphore_signal(barrier, inc=1, device_id={"occ": lax.rem(mine + off, 8)}, device_id_type=MESH)

    labs = lab_ref[...].reshape(1, nv)
    mylab = virs_ref[me * la]
    jocc = [occ_ref[2 * mine + j] for j in range(2)]

    quarter = lax.broadcasted_iota(jnp.int32, (la, nv), 1) // WIN

    def spread(part):
        part = part + pltpu.roll(part, 2 * WIN, 1)
        return part + pltpu.roll(part, WIN, 1)

    def pack(j):
        both = []
        for kp in range(2):
            total = None
            for kk in range(4):
                k = 4 * kp + kk
                want = kocc_ref[k] ^ jocc[j] ^ mylab
                part = spread(jnp.where(labs == want, w_ref[k, :, j, :].astype(jnp.float32), 0.0))
                total = part if total is None else jnp.where(quarter >= kk, part, total)
            both.append(total)
        panels[j, me] = jnp.concatenate(both, axis=0).astype(jnp.bfloat16)

    copies = []
    spans = [[(0, 48), (48, 80)], [(0, 32), (32, 80)]]

    def halves(j, h, turn):
        low, high = spans[j][h]
        middle = low + (32 if high - low == 48 and turn else 16)
        return (low, middle), (middle, high)

    def send(j, h, block, rows, step, slot):
        p, q = here[h]
        ref = panels.at[j, at(h, p + block[0], q + block[1]), pl.ds(rows[0], rows[1] - rows[0])]
        c = pltpu.make_async_remote_copy(
            src_ref=ref, dst_ref=ref, send_sem=send_sem.at[j, h, slot], recv_sem=recv_sem.at[j, h, slot],
            device_id={"vir": at(h, p + step[0], q + step[1])}, device_id_type=MESH)
        c.start()
        copies.append(c)

    def arrived(j, h, block, rows, slot):
        p, q = here[h]
        ref = panels.at[j, at(h, p + block[0], q + block[1]), pl.ds(rows[0], rows[1] - rows[0])]
        pltpu.make_async_remote_copy(
            src_ref=ref, dst_ref=ref, send_sem=send_sem.at[j, h, slot], recv_sem=recv_sem.at[j, h, slot],
            device_id={"vir": me}, device_id_type=MESH).wait_recv()

    def second(j, h, d):
        send(j, h, (d, 0), spans[j][h], (0, 1), 4 + 4 * d)
        send(j, h, (d, 0), spans[j][h], (0, -1), 5 + 4 * d)

    def start(j):
        for h in range(2):
            send(j, h, (0, 0), spans[j][h], (1, 0), 0)
            send(j, h, (0, 0), spans[j][h], (-1, 0), 1)
            second(j, h, 0)

    def first_axis(j):
        for h in range(2):
            low, high = halves(j, h, 0)
            arrived(j, h, (-1, 0), spans[j][h], 0)
            send(j, h, (-1, 0), low, (1, 0), 2)
            second(j, h, 3)
            arrived(j, h, (1, 0), spans[j][h], 1)
            send(j, h, (1, 0), high, (-1, 0), 3)
            second(j, h, 1)

    def opposite(j):
        for h in range(2):
            low, high = halves(j, h, 0)
            arrived(j, h, (-2, 0), low, 2)
            arrived(j, h, (-2, 0), high, 3)
            second(j, h, 2)

    def relay(j, d):
        b = d if d < 2 else d - 4
        for h in range(2):
            low, high = halves(j, h, d % 2)
            arrived(j, h, (b, -1), spans[j][h], 4 + 4 * d)
            send(j, h, (b, -1), low, (0, 1), 6 + 4 * d)
            arrived(j, h, (b, 1), spans[j][h], 5 + 4 * d)
            send(j, h, (b, 1), high, (0, -1), 7 + 4 * d)

    def complete(j):
        for h in range(2):
            for d in range(4):
                b = d if d < 2 else d - 4
                low, high = halves(j, h, d % 2)
                arrived(j, h, (b, 2), low, 6 + 4 * d)
                arrived(j, h, (b, 2), high, 7 + 4 * d)

    rows = la * nk

    def prepare(low, high):
        @pl.loop(low, high)
        def _(i):
            parts = []
            for s in range(2):
                orb = tab[ORDER + 2 * i + s]
                moved = jnp.dot(rowp[...], amp[orb].reshape(rows, nv), preferred_element_type=jnp.float32)
                left = occ_ref[orb] ^ mylab
                parts.append([
                    jnp.where(labs == (left ^ kocc_ref[k]), moved[k * la:(k + 1) * la], 0.0)
                    for k in range(nk)])
            for k in range(nk):
                tk[k, pl.ds(pl.multiple_of(2 * la * i, 16), 2 * la), :] = jnp.concatenate(
                    [parts[0][k], parts[1][k]], axis=0).astype(jnp.bfloat16)

    def order_rows(j):
        @pl.loop(0, 8)
        def _(v):
            one = panels[j, 2 * v].astype(jnp.float32)
            two = panels[j, 2 * v + 1].astype(jnp.float32)
            for kp in range(2):
                wk[j, kp, pl.ds(pl.multiple_of(2 * la * v, 16), 2 * la), :] = jnp.concatenate(
                    [one[kp * la:(kp + 1) * la], two[kp * la:(kp + 1) * la]], axis=0).astype(jnp.bfloat16)

    def multiply(j, low, high):
        @pl.loop(low, high)
        def _(kk):
            lanes = pl.ds(pl.multiple_of(128 * kk, 128), 256)
            t = jnp.concatenate([tk[kk], tk[4 + kk]], axis=1)
            w = jnp.concatenate([wk[j, 0, :, lanes], wk[j, 1, :, lanes]], axis=0)
            acc[kk] = jnp.dot(t, w, preferred_element_type=jnp.float32)

    def combine(j):
        whole = acc[0]
        for kk in range(1, 4):
            whole = whole + pltpu.roll(acc[kk], 256 - 32 * kk, 1)
        wide = lax.broadcasted_iota(jnp.int32, whole.shape, 1)
        whole = jnp.where(wide < WIN, whole, 0.0).astype(jnp.bfloat16).astype(jnp.float32)
        cw[j] = whole.reshape(batch, la, 256)
        spot = lax.broadcasted_iota(jnp.int32, (batch * la, 128), 1)
        for r in range(4):
            width = 128 if r < 3 else 256
            total = None
            for g in range(3):
                piece = whole[g * la:, :width]
                if g != r:
                    piece = pltpu.roll(piece, (la * (g - r)) % width, 1)
                piece = piece[:, :128]
                if g:
                    piece = jnp.concatenate([piece, jnp.zeros((g * la, 128), jnp.float32)], axis=0)
                total = piece if g == 0 else jnp.where(spot >= g * la, piece, total)
            comb[4 * j + r] = total.reshape(batch, la, 128)

    def message(j, v):
        base = tab[BEGIN + (jocc[j] ^ virs_ref[v * la] ^ mylab)]
        parts = [comb[4 * j + lax.rem(v, 4), base + 3 * q] for q in range(groups)]
        return jnp.concatenate(parts, axis=0).astype(jnp.bfloat16)

    def far_copy(j, off, v, source):
        return pltpu.make_async_remote_copy(
            src_ref=far.at[j, v], dst_ref=near.at[j, source], send_sem=far_send.at[j, off],
            recv_sem=far_recv.at[j, off], device_id={"vir": v}, device_id_type=MESH)

    def send_far(j):
        @pl.loop(1, 16)
        def _(off):
            v = beside(off)
            far[j, v] = message(j, v)
            far_copy(j, off, v, me).start()

    def take(j, source, value):
        nearf[source, groups * j:groups * (j + 1)] = value.astype(jnp.float32).reshape(groups, la, 128)

    def take_far(j):
        take(j, me, message(j, me))

        @pl.loop(1, 16)
        def _(off):
            source = behind(off)
            far_copy(j, off, source, source).wait_recv()
            take(j, source, near[j, source])

    def windows(j, o):
        wins = []
        for s in range(2):
            orb = 2 * o + s
            want = occ_ref[orb] ^ mylab ^ jocc[j]
            row = groups * j + tab[GROUP + orb]
            stack = [nearf[tab[BLOCK + 4 * want + d], row] for d in range(4)]
            stack = jnp.concatenate(stack + [jnp.zeros((96, 128), jnp.float32)], axis=0).T
            for m in range(3):
                turned[s, m] = stack[m * la:(m + 1) * la]
            wins.append(turned[s, tab[MEMBER + orb]])
        rest = wins[0][:, 128:] + pltpu.roll(wins[1][:, 128:], 32, 1)
        return jnp.concatenate(
            [wins[0][:, :128], wins[1][:, :128], rest, jnp.zeros((8, 128), jnp.float32)], axis=0).astype(jnp.bfloat16)

    def occ_copy(j, off, o, source):
        return pltpu.make_async_remote_copy(
            src_ref=pack_out.at[j, o], dst_ref=pack_in.at[j, source], send_sem=occ_send.at[j, off],
            recv_sem=occ_recv.at[j, off], device_id={"occ": o}, device_id_type=MESH)

    def send_occ(j):
        @pl.loop(1, 8)
        def _(off):
            o = lax.rem(mine + off, 8)
            pack_out[j, o] = windows(j, o)
            occ_copy(j, off, o, mine).start()

        pack_in[j, mine] = windows(j, mine)

    thin = lax.broadcasted_iota(jnp.int32, (la, 128), 1) < 32
    none = jnp.zeros((la, 128), jnp.float32)

    def finish(i2, o):
        orb = 2 * o + i2
        back = pack_in[i2, o].astype(jnp.float32)
        rest = back[2 * la:3 * la]
        for j in range(2):
            if j:
                rest = pltpu.roll(rest, 96, 1)
            own = cw[j, tab[PLACE + orb]]
            low = own[:, :128] + back[j * la:(j + 1) * la]
            high = own[:, 128:] + jnp.where(thin, rest, 0.0)
            row = spread(jnp.concatenate([low, high, none, none, none], axis=1))
            want = occ_ref[orb] ^ mylab ^ jocc[j]
            out_ref[orb, j] = jnp.where(labs == want, row, 0.0).astype(jnp.bfloat16)

    def finish_all(i2):
        finish(i2, mine)

        @pl.loop(1, 8)
        def _(off):
            source = lax.rem(mine + 8 - off, 8)
            occ_copy(i2, off, source, source).wait_recv()
            finish(i2, source)

    pack(0)
    pl.semaphore_wait(barrier, 22)
    start(0)
    pack(1)
    r = lax.broadcasted_iota(jnp.int32, (rows, rows), 0)
    c = lax.broadcasted_iota(jnp.int32, (rows, rows), 1)
    rowp[...] = (c == lax.rem(r, la) * nk + r // la).astype(jnp.float32).astype(jnp.bfloat16)
    for c in amp_copies:
        c.wait()
    first_axis(0)
    prepare(0, 2)
    relay(0, 0)
    opposite(0)
    prepare(2, 5)
    relay(0, 3)
    relay(0, 1)
    start(1)
    prepare(5, 8)
    relay(0, 2)
    first_axis(1)
    complete(0)
    order_rows(0)
    relay(1, 0)
    opposite(1)
    multiply(0, 0, 4)
    relay(1, 3)
    relay(1, 1)
    combine(0)
    send_far(0)
    relay(1, 2)
    complete(1)
    order_rows(1)
    multiply(1, 0, 4)
    combine(1)
    send_far(1)
    take_far(0)
    send_occ(0)
    take_far(1)
    send_occ(1)
    finish_all(0)
    finish_all(1)
    for c in copies:
        c.wait_send()
    for j in range(2):
        @pl.loop(1, 16)
        def _(off):
            far_copy(j, off, beside(off), me).wait_send()

        @pl.loop(1, 8)
        def _(off):
            occ_copy(j, off, lax.rem(mine + off, 8), mine).wait_send()


def residual_rows(groups, collective, amplitude, integral, occ_irrep, kocc_irrep, vir_irrep, table):
    batch, la, nk, nv = amplitude.shape
    rows = groups * la
    smem, vmem = pl.BlockSpec(memory_space=pltpu.SMEM), pl.BlockSpec(memory_space=pltpu.VMEM)
    return pl.pallas_call(
        functools.partial(cycle_kernel, groups),
        out_shape=jax.ShapeDtypeStruct((batch, 2, la, nv), jnp.bfloat16),
        in_specs=[pl.BlockSpec(memory_space=pl.ANY), vmem, smem, smem, vmem, smem, smem],
        out_specs=vmem,
        scratch_shapes=[
            pltpu.VMEM((batch, la, nk, nv), jnp.bfloat16),
            pltpu.VMEM((2, 16, 2 * la, 640), jnp.bfloat16),
            pltpu.VMEM((nk, batch * la, nv), jnp.bfloat16),
            pltpu.VMEM((2, 2, nv, 640), jnp.bfloat16),
            pltpu.VMEM((4, batch * la, 256), jnp.float32),
            pltpu.VMEM((la * nk, la * nk), jnp.bfloat16),
            pltpu.VMEM((2, batch, la, 256), jnp.float32),
            pltpu.VMEM((8, batch, la, 128), jnp.float32),
            pltpu.VMEM((2, 16, rows, 128), jnp.bfloat16),
            pltpu.VMEM((2, 16, rows, 128), jnp.bfloat16),
            pltpu.VMEM((16, 2 * groups, la, 128), jnp.float32),
            pltpu.VMEM((2, 3, la, 256), jnp.float32),
            pltpu.VMEM((2, 8, 128, 128), jnp.bfloat16),
            pltpu.VMEM((2, 8, 128, 128), jnp.bfloat16),
            pltpu.SemaphoreType.DMA((batch // 2,)),
            pltpu.SemaphoreType.DMA((2, 2, 20)),
            pltpu.SemaphoreType.DMA((2, 2, 20)),
            pltpu.SemaphoreType.DMA((2, 16)),
            pltpu.SemaphoreType.DMA((2, 16)),
            pltpu.SemaphoreType.DMA((2, 8)),
            pltpu.SemaphoreType.DMA((2, 8)),
        ],
        compiler_params=pltpu.CompilerParams(
            collective_id=collective, has_side_effects=True, vmem_limit_bytes=56 * 1024 * 1024),
        name="cycle_residual",
    )(amplitude, integral, occ_irrep, kocc_irrep, vir_irrep, vir_irrep, table)


def shards(amplitude, integral, occ_irrep, kocc_irrep, vir_irrep):
    table = make_table(2, occ_irrep, vir_irrep)
    args = (amplitude, integral, occ_irrep, kocc_irrep, vir_irrep)
    rows = lax.cond(
        table[MOST] <= FEW,
        lambda *a: residual_rows(2, 0, *a, table),
        lambda *a: residual_rows(6, 1, *a, make_table(6, occ_irrep, vir_irrep)),
        *args,
    )
    return jnp.transpose(rows, (0, 2, 1, 3))


def solution(mesh):
    in_specs = (P(None, "vir", None, None), P(None, "vir", "occ", None), P(), P(), P())
    out_specs = P(None, "vir", "occ", None)
    return jax.shard_map(shards, mesh=mesh, in_specs=in_specs, out_specs=out_specs, check_vma=False)
```

```python
import functools
import jax
import jax.numpy as jnp
from jax import lax
from jax.experimental import pallas as pl
from jax.experimental.pallas import tpu as pltpu
from jax.sharding import PartitionSpec as P

WIN = 160
FEW, FEW_ODD = 6, 3
MESH = pl.DeviceIdType.MESH
ORDER, PLACE, BEGIN, BLOCK, GROUP, MEMBER, MOST = 0, 16, 32, 40, 72, 88, 104
ODD_ORDER, ODD_BEGIN, ODD_GROUP, ODD_MEMBER = 128, 136, 144, 152


def table_kernel(groups, occ_ref, virs_ref, tab):
    batch = occ_ref.shape[0]
    la = virs_ref.shape[0] // 16
    occ = [occ_ref[i] for i in range(batch)]
    places = [jnp.int32(0)] * batch
    for i in range(batch):
        for o in range(i):
            before = (occ[o] <= occ[i]).astype(jnp.int32)
            places[i] = places[i] + before
            places[o] = places[o] + (1 - before)
    below = []
    for r in range(8):
        total = jnp.int32(0)
        for o in range(batch):
            total = total + (occ[o] < r).astype(jnp.int32)
        below.append(total)
    below.append(jnp.int32(batch))
    odd_below = []
    for r in range(8):
        total = jnp.int32(0)
        for o in range(1, batch, 2):
            total = total + (occ[o] < r).astype(jnp.int32)
        odd_below.append(total)
    odd_below.append(jnp.int32(batch // 2))
    odd_groups = groups // 2
    excess = jnp.int32(0)
    for r in range(8):
        excess = jnp.maximum(excess, below[r + 1] - below[r] - FEW)
        excess = jnp.maximum(excess, odd_below[r + 1] - odd_below[r] - FEW_ODD)
        tab[BEGIN + r] = jnp.minimum(below[r], max(batch - 3 * groups, 0))
        tab[ODD_BEGIN + r] = jnp.minimum(odd_below[r], max(batch // 2 - 3 * odd_groups, 0))
        for d in range(4):
            tab[BLOCK + 4 * r + d] = jnp.int32(0)
    for i in range(MOST, 128):
        tab[i] = excess
    for v in range(16):
        tab[BLOCK + 4 * virs_ref[la * v] + v % 4] = jnp.int32(v)

    def enter(slot, count, group_at, member_at):
        group = jnp.int32(0)
        for q in range(1, count):
            group = group + (slot >= 3 * q).astype(jnp.int32)
        tab[group_at] = group
        tab[member_at] = slot - 3 * group

    for i in range(batch):
        tab[PLACE + i] = places[i]
        tab[ORDER + places[i]] = jnp.int32(i)
        enter(places[i] - tab[BEGIN + occ[i]], groups, GROUP + i, MEMBER + i)
    for t in range(batch // 2):
        place = jnp.int32(0)
        for o in range(batch // 2):
            if o != t:
                a, b = occ[2 * o + 1], occ[2 * t + 1]
                place = place + ((a <= b) if o < t else (a < b)).astype(jnp.int32)
        tab[ODD_ORDER + place] = jnp.int32(t)
        enter(place - tab[ODD_BEGIN + occ[2 * t + 1]], odd_groups, ODD_GROUP + t, ODD_MEMBER + t)
    for i in range(160, 256):
        tab[i] = jnp.int32(0)


def make_table(groups, occ_irrep, vir_irrep):
    smem = pl.BlockSpec(memory_space=pltpu.SMEM)
    return pl.pallas_call(
        functools.partial(table_kernel, groups),
        out_shape=jax.ShapeDtypeStruct((256,), jnp.int32),
        in_specs=[smem, smem],
        out_specs=smem,
        name="make_table",
    )(occ_irrep, vir_irrep)


def cycle_kernel(groups, amp_ref, w_ref, occ_ref, kocc_ref, lab_ref, virs_ref, tab, out_ref,
                 amp, panels, tk, wk, acc, rowp, cw, comb, far, near, nearf, turned, pack_out, pack_in, odd, odd_comb,
                 amp_sem, send_sem, recv_sem, far_send, far_recv, occ_send, occ_recv):
    me = lax.axis_index("vir")
    mine = lax.axis_index("occ")
    z, x = me // 4, lax.rem(me, 4)
    batch, la, nk, nv = amp.shape
    pairs = batch // 2
    here = [(x, z), (z, x)]

    amp_copies = [
        pltpu.make_async_copy(amp_ref.at[pl.ds(2 * i, 2)], amp.at[pl.ds(2 * i, 2)], amp_sem.at[i])
        for i in range(pairs)]
    for c in amp_copies:
        c.start()

    def at(h, p, q):
        p, q = lax.rem(p + 8, 4), lax.rem(q + 8, 4)
        return q * 4 + p if h == 0 else p * 4 + q

    def beside(off):
        return lax.rem(z + off // 4, 4) * 4 + lax.rem(x + lax.rem(off, 4), 4)

    def behind(off):
        return lax.rem(z + 4 - off // 4, 4) * 4 + lax.rem(x + 4 - lax.rem(off, 4), 4)

    barrier = pltpu.get_barrier_semaphore()

    @pl.loop(1, 16)
    def _(off):
        pl.semaphore_signal(barrier, inc=1, device_id={"vir": beside(off)}, device_id_type=MESH)

    @pl.loop(1, 8)
    def _(off):
        pl.semaphore_signal(barrier, inc=1, device_id={"occ": lax.rem(mine + off, 8)}, device_id_type=MESH)

    labs = lab_ref[...].reshape(1, nv)
    mylab = virs_ref[me * la]
    jocc = [occ_ref[2 * mine + j] for j in range(2)]

    quarter = lax.broadcasted_iota(jnp.int32, (la, nv), 1) // WIN

    def spread(part):
        part = part + pltpu.roll(part, 2 * WIN, 1)
        return part + pltpu.roll(part, WIN, 1)

    def pack(j):
        both = []
        for kp in range(2):
            total = None
            for kk in range(4):
                k = 4 * kp + kk
                want = kocc_ref[k] ^ jocc[j] ^ mylab
                part = spread(jnp.where(labs == want, w_ref[k, :, j, :].astype(jnp.float32), 0.0))
                total = part if total is None else jnp.where(quarter >= kk, part, total)
            both.append(total)
        panels[j, me] = jnp.concatenate(both, axis=0).astype(jnp.bfloat16)

    copies = []
    full = (0, 2 * la)

    def halves(h, turn):
        middle = 48 if (h + turn) % 2 else 32
        return (0, middle), (middle, 2 * la)

    def send(h, block, rows, step, slot):
        p, q = here[h]
        ref = panels.at[h, at(h, p + block[0], q + block[1]), pl.ds(rows[0], rows[1] - rows[0])]
        c = pltpu.make_async_remote_copy(
            src_ref=ref, dst_ref=ref, send_sem=send_sem.at[h, slot], recv_sem=recv_sem.at[h, slot],
            device_id={"vir": at(h, p + step[0], q + step[1])}, device_id_type=MESH)
        c.start()
        copies.append(c)

    def arrived(h, block, rows, slot):
        p, q = here[h]
        ref = panels.at[h, at(h, p + block[0], q + block[1]), pl.ds(rows[0], rows[1] - rows[0])]
        pltpu.make_async_remote_copy(
            src_ref=ref, dst_ref=ref, send_sem=send_sem.at[h, slot], recv_sem=recv_sem.at[h, slot],
            device_id={"vir": me}, device_id_type=MESH).wait_recv()

    def second(h, d):
        send(h, (d, 0), full, (0, 1), 4 + 4 * d)
        send(h, (d, 0), full, (0, -1), 5 + 4 * d)

    def start(h):
        send(h, (0, 0), full, (1, 0), 0)
        send(h, (0, 0), full, (-1, 0), 1)
        second(h, 0)

    def first_axis():
        for h in range(2):
            low, high = halves(h, 0)
            arrived(h, (-1, 0), full, 0)
            send(h, (-1, 0), low, (1, 0), 2)
            second(h, 3)
            arrived(h, (1, 0), full, 1)
            send(h, (1, 0), high, (-1, 0), 3)
            second(h, 1)

    def opposite():
        for h in range(2):
            low, high = halves(h, 0)
            arrived(h, (-2, 0), low, 2)
            arrived(h, (-2, 0), high, 3)
            second(h, 2)

    def relay(d):
        b = d if d < 2 else d - 4
        for h in range(2):
            low, high = halves(h, d % 2)
            arrived(h, (b, -1), full, 4 + 4 * d)
            send(h, (b, -1), low, (0, 1), 6 + 4 * d)
            arrived(h, (b, 1), full, 5 + 4 * d)
            send(h, (b, 1), high, (0, -1), 7 + 4 * d)

    def complete(h):
        for d in range(4):
            b = d if d < 2 else d - 4
            low, high = halves(h, d % 2)
            arrived(h, (b, 2), low, 6 + 4 * d)
            arrived(h, (b, 2), high, 7 + 4 * d)

    rows = la * nk

    def prepare(low, high):
        @pl.loop(low, high)
        def _(i):
            parts = []
            for s in range(2):
                orb = tab[ORDER + 2 * i + s]
                moved = jnp.dot(rowp[...], amp[orb].reshape(rows, nv), preferred_element_type=jnp.float32)
                left = occ_ref[orb] ^ mylab
                parts.append([
                    jnp.where(labs == (left ^ kocc_ref[k]), moved[k * la:(k + 1) * la], 0.0)
                    for k in range(nk)])
            for k in range(nk):
                tk[k, pl.ds(pl.multiple_of(2 * la * i, 16), 2 * la), :] = jnp.concatenate(
                    [parts[0][k], parts[1][k]], axis=0).astype(jnp.bfloat16)

    def order_rows(j):
        @pl.loop(0, 8)
        def _(v):
            one = panels[j, 2 * v].astype(jnp.float32)
            two = panels[j, 2 * v + 1].astype(jnp.float32)
            for kp in range(2):
                wk[j, kp, pl.ds(pl.multiple_of(2 * la * v, 16), 2 * la), :] = jnp.concatenate(
                    [one[kp * la:(kp + 1) * la], two[kp * la:(kp + 1) * la]], axis=0).astype(jnp.bfloat16)

    def multiply(j, low, high):
        @pl.loop(low, high)
        def _(kk):
            lanes = pl.ds(pl.multiple_of(128 * kk, 128), 256)
            t = jnp.concatenate([tk[kk], tk[4 + kk]], axis=1)
            w = jnp.concatenate([wk[j, 0, :, lanes], wk[j, 1, :, lanes]], axis=0)
            acc[kk] = jnp.dot(t, w, preferred_element_type=jnp.float32)

    def collect(j):
        whole = acc[0]
        for kk in range(1, 4):
            whole = whole + pltpu.roll(acc[kk], 256 - 32 * kk, 1)
        wide = lax.broadcasted_iota(jnp.int32, whole.shape, 1)
        whole = jnp.where(wide < WIN, whole, 0.0).astype(jnp.bfloat16).astype(jnp.float32)
        cw[j] = whole.reshape(batch, la, 256)
        return whole

    def mix(whole, r):
        spot = lax.broadcasted_iota(jnp.int32, (whole.shape[0], 128), 1)
        width = 128 if r < 3 else 256
        total = None
        for g in range(3):
            piece = whole[g * la:, :width]
            if g != r:
                piece = pltpu.roll(piece, (la * (g - r)) % width, 1)
            piece = piece[:, :128]
            if g:
                piece = jnp.concatenate([piece, jnp.zeros((g * la, 128), jnp.float32)], axis=0)
            total = piece if g == 0 else jnp.where(spot >= g * la, piece, total)
        return total.reshape(whole.shape[0] // la, la, 128)

    def even_message(v):
        base = tab[BEGIN + (jocc[0] ^ virs_ref[v * la] ^ mylab)]
        parts = [comb[lax.rem(v, 4), base + 3 * q] for q in range(groups)]
        return jnp.concatenate(parts, axis=0).astype(jnp.bfloat16)

    def odd_message(v):
        parts = []
        for s in range(2):
            base = tab[ODD_BEGIN + (jocc[s] ^ virs_ref[v * la] ^ mylab)]
            parts += [odd_comb[4 * s + lax.rem(v, 4), base + 3 * q] for q in range(groups // 2)]
        return jnp.concatenate(parts, axis=0).astype(jnp.bfloat16)

    messages = [even_message, odd_message]

    def far_copy(j, off, v, source):
        return pltpu.make_async_remote_copy(
            src_ref=far.at[j, v], dst_ref=near.at[j, source], send_sem=far_send.at[j, off],
            recv_sem=far_recv.at[j, off], device_id={"vir": v}, device_id_type=MESH)

    def send_far(j):
        @pl.loop(1, 16)
        def _(off):
            v = beside(off)
            far[j, v] = messages[j](v)
            far_copy(j, off, v, me).start()

    def take(j, source, value):
        nearf[j, source] = value.astype(jnp.float32).reshape(groups, la, 128)

    def take_far(j):
        take(j, me, messages[j](me))

        @pl.loop(1, 16)
        def _(off):
            source = behind(off)
            far_copy(j, off, source, source).wait_recv()
            take(j, source, near[j, source])

    def window(j, s, want, row, member):
        stack = [nearf[j, tab[BLOCK + 4 * want + d], row] for d in range(4)]
        stack = jnp.concatenate(stack + [jnp.zeros((96, 128), jnp.float32)], axis=0).T
        for m in range(3):
            turned[s, m] = stack[m * la:(m + 1) * la]
        return turned[s, member]

    def join(wins):
        rest = wins[0][:, 128:] + pltpu.roll(wins[1][:, 128:], 32, 1)
        return jnp.concatenate(
            [wins[0][:, :128], wins[1][:, :128], rest, jnp.zeros((8, 128), jnp.float32)], axis=0).astype(jnp.bfloat16)

    def even_windows(o):
        wins = []
        for s in range(2):
            orb = 2 * o + s
            wins.append(window(0, s, occ_ref[orb] ^ mylab ^ jocc[0], tab[GROUP + orb], tab[MEMBER + orb]))
        return join(wins)

    def odd_windows(o):
        return join([cw[1, tab[PLACE + 2 * o + s]] for s in range(2)])

    def occ_copy(j, off, o, source):
        return pltpu.make_async_remote_copy(
            src_ref=pack_out.at[j, o], dst_ref=pack_in.at[j, source], send_sem=occ_send.at[j, off],
            recv_sem=occ_recv.at[j, off], device_id={"occ": o}, device_id_type=MESH)

    def send_occ(j, make):
        @pl.loop(1, 8)
        def _(off):
            o = lax.rem(mine + off, 8)
            pack_out[j, o] = make(o)
            occ_copy(j, off, o, mine).start()

        pack_in[j, mine] = make(mine)

    thin = lax.broadcasted_iota(jnp.int32, (la, 128), 1) < 32
    none = jnp.zeros((la, 128), jnp.float32)

    def part_of(j, o):
        back = pack_in[j, o].astype(jnp.float32)
        rest = back[2 * la:3 * la]
        return [
            jnp.concatenate([back[:la], jnp.where(thin, rest, 0.0)], axis=1),
            jnp.concatenate([back[la:2 * la], jnp.where(thin, pltpu.roll(rest, 96, 1), 0.0)], axis=1)]

    def wait_occ(j, then):
        then(mine)

        @pl.loop(1, 8)
        def _(off):
            source = lax.rem(mine + 8 - off, 8)
            occ_copy(j, off, source, source).wait_recv()
            then(source)

    def finish(orb, mirrors):
        for j in range(2):
            row = cw[j, tab[PLACE + orb]] + mirrors[j]
            row = spread(jnp.concatenate([row, none, none, none], axis=1))
            want = occ_ref[orb] ^ mylab ^ jocc[j]
            out_ref[orb, j] = jnp.where(labs == want, row, 0.0).astype(jnp.bfloat16)

    def keep_odd(o):
        odd[0, o], odd[1, o] = part_of(1, o)

    def finish_odd():
        @pl.loop(0, 8)
        def _(o):
            orb = 2 * o + 1
            finish(orb, [
                window(1, s, occ_ref[orb] ^ mylab ^ jocc[s], groups // 2 * s + tab[ODD_GROUP + o], tab[ODD_MEMBER + o])
                for s in range(2)])

    pack(0)
    pl.semaphore_wait(barrier, 22)
    start(0)
    pack(1)
    start(1)
    r = lax.broadcasted_iota(jnp.int32, (rows, rows), 0)
    c = lax.broadcasted_iota(jnp.int32, (rows, rows), 1)
    rowp[...] = (c == lax.rem(r, la) * nk + r // la).astype(jnp.float32).astype(jnp.bfloat16)
    for c in amp_copies:
        c.wait()
    prepare(0, 1)
    first_axis()
    prepare(1, 2)
    relay(0)
    prepare(2, 3)
    opposite()
    prepare(3, 5)
    relay(3)
    prepare(5, 6)
    relay(1)
    prepare(6, 8)
    relay(2)
    complete(1)
    order_rows(1)
    multiply(1, 0, 4)
    collect(1)
    send_occ(1, odd_windows)
    complete(0)
    order_rows(0)
    multiply(0, 0, 4)
    whole = collect(0)
    for q in range(4):
        comb[q] = mix(whole, q)
    send_far(0)

    wait_occ(1, keep_odd)
    for s in range(2):
        sorted_odd = jnp.concatenate([odd[s, tab[ODD_ORDER + t]] for t in range(batch // 2)], axis=0)
        for q in range(4):
            odd_comb[4 * s + q] = mix(sorted_odd, q)
    send_far(1)
    take_far(0)
    send_occ(0, even_windows)
    take_far(1)
    finish_odd()
    wait_occ(0, lambda o: finish(2 * o, part_of(0, o)))
    for c in copies:
        c.wait_send()
    for j in range(2):
        @pl.loop(1, 16)
        def _(off):
            far_copy(j, off, beside(off), me).wait_send()

        @pl.loop(1, 8)
        def _(off):
            occ_copy(j, off, lax.rem(mine + off, 8), mine).wait_send()


def residual_rows(groups, collective, amplitude, integral, occ_irrep, kocc_irrep, vir_irrep, table):
    batch, la, nk, nv = amplitude.shape
    rows = groups * la
    smem, vmem = pl.BlockSpec(memory_space=pltpu.SMEM), pl.BlockSpec(memory_space=pltpu.VMEM)
    return pl.pallas_call(
        functools.partial(cycle_kernel, groups),
        out_shape=jax.ShapeDtypeStruct((batch, 2, la, nv), jnp.bfloat16),
        in_specs=[pl.BlockSpec(memory_space=pl.ANY), vmem, smem, smem, vmem, smem, smem],
        out_specs=vmem,
        scratch_shapes=[
            pltpu.VMEM((batch, la, nk, nv), jnp.bfloat16),
            pltpu.VMEM((2, 16, 2 * la, 640), jnp.bfloat16),
            pltpu.VMEM((nk, batch * la, nv), jnp.bfloat16),
            pltpu.VMEM((2, 2, nv, 640), jnp.bfloat16),
            pltpu.VMEM((4, batch * la, 256), jnp.float32),
            pltpu.VMEM((la * nk, la * nk), jnp.bfloat16),
            pltpu.VMEM((2, batch, la, 256), jnp.float32),
            pltpu.VMEM((4, batch, la, 128), jnp.float32),
            pltpu.VMEM((2, 16, rows, 128), jnp.bfloat16),
            pltpu.VMEM((2, 16, rows, 128), jnp.bfloat16),
            pltpu.VMEM((2, 16, groups, la, 128), jnp.float32),
            pltpu.VMEM((2, 3, la, 256), jnp.float32),
            pltpu.VMEM((2, 8, 128, 128), jnp.bfloat16),
            pltpu.VMEM((2, 8, 128, 128), jnp.bfloat16),
            pltpu.VMEM((2, 8, la, 256), jnp.float32),
            pltpu.VMEM((8, 8, la, 128), jnp.float32),
            pltpu.SemaphoreType.DMA((batch // 2,)),
            pltpu.SemaphoreType.DMA((2, 20)),
            pltpu.SemaphoreType.DMA((2, 20)),
            pltpu.SemaphoreType.DMA((2, 16)),
            pltpu.SemaphoreType.DMA((2, 16)),
            pltpu.SemaphoreType.DMA((2, 8)),
            pltpu.SemaphoreType.DMA((2, 8)),
        ],
        compiler_params=pltpu.CompilerParams(
            collective_id=collective, has_side_effects=True, vmem_limit_bytes=56 * 1024 * 1024),
        name="cycle_residual",
    )(amplitude, integral, occ_irrep, kocc_irrep, vir_irrep, vir_irrep, table)


def shards(amplitude, integral, occ_irrep, kocc_irrep, vir_irrep):
    table = make_table(2, occ_irrep, vir_irrep)
    args = (amplitude, integral, occ_irrep, kocc_irrep, vir_irrep)
    rows = lax.cond(
        table[MOST] <= 0,
        lambda *a: residual_rows(2, 0, *a, table),
        lambda *a: residual_rows(6, 1, *a, make_table(6, occ_irrep, vir_irrep)),
        *args,
    )
    return jnp.transpose(rows, (0, 2, 1, 3))


def solution(mesh):
    in_specs = (P(None, "vir", None, None), P(None, "vir", "occ", None), P(), P(), P())
    out_specs = P(None, "vir", "occ", None)
    return jax.shard_map(shards, mesh=mesh, in_specs=in_specs, out_specs=out_specs, check_vma=False)
```

```python
import functools
import jax
import jax.numpy as jnp
from jax import lax
from jax.experimental import pallas as pl
from jax.experimental.pallas import tpu as pltpu
from jax.sharding import PartitionSpec as P

WIN = 160
FEW = 6
MESH = pl.DeviceIdType.MESH
ORDER, PLACE, BEGIN, BLOCK, GROUP, MEMBER, MOST = 0, 16, 32, 40, 72, 88, 104


def table_kernel(groups, occ_ref, virs_ref, tab):
    batch = occ_ref.shape[0]
    la = virs_ref.shape[0] // 16
    occ = [occ_ref[i] for i in range(batch)]
    places = [jnp.int32(0)] * batch
    for i in range(batch):
        for o in range(i):
            before = (occ[o] <= occ[i]).astype(jnp.int32)
            places[i] = places[i] + before
            places[o] = places[o] + (1 - before)
    below = []
    for r in range(8):
        total = jnp.int32(0)
        for o in range(batch):
            total = total + (occ[o] < r).astype(jnp.int32)
        below.append(total)
    below.append(jnp.int32(batch))
    most = jnp.int32(0)
    for r in range(8):
        most = jnp.maximum(most, below[r + 1] - below[r])
        tab[BEGIN + r] = jnp.minimum(below[r], max(batch - 3 * groups, 0))
        for d in range(4):
            tab[BLOCK + 4 * r + d] = jnp.int32(0)
    tab[MOST] = most
    for v in range(16):
        tab[BLOCK + 4 * virs_ref[la * v] + v % 4] = jnp.int32(v)
    for i in range(batch):
        tab[PLACE + i] = places[i]
        tab[ORDER + places[i]] = jnp.int32(i)
        slot = places[i] - tab[BEGIN + occ[i]]
        group = jnp.int32(0)
        for q in range(1, groups):
            group = group + (slot >= 3 * q).astype(jnp.int32)
        tab[GROUP + i] = group
        tab[MEMBER + i] = slot - 3 * group


def make_table(groups, occ_irrep, vir_irrep):
    smem = pl.BlockSpec(memory_space=pltpu.SMEM)
    return pl.pallas_call(
        functools.partial(table_kernel, groups),
        out_shape=jax.ShapeDtypeStruct((105,), jnp.int32),
        in_specs=[smem, smem],
        out_specs=smem,
        name="make_table",
    )(occ_irrep, vir_irrep)


def cycle_kernel(groups, amp_ref, w_ref, occ_ref, kocc_ref, lab_ref, virs_ref, tab, out_ref,
                 amp, panels, tk, row_wk, wk, acc, rowp, cw, comb, far, near, nearf, turned, pack_out, pack_in,
                 amp_sem, send_sem, recv_sem, far_send, far_recv, occ_send, occ_recv):
    me = lax.axis_index("vir")
    mine = lax.axis_index("occ")
    z, x = me // 4, lax.rem(me, 4)
    batch, la, nk, nv = amp.shape
    pairs = batch // 2
    here = [(x, z), (z, x)]

    amp_copies = [
        pltpu.make_async_copy(amp_ref.at[pl.ds(2 * i, 2)], amp.at[pl.ds(2 * i, 2)], amp_sem.at[i])
        for i in range(pairs)]
    for c in amp_copies:
        c.start()

    def at(h, p, q):
        p, q = lax.rem(p + 8, 4), lax.rem(q + 8, 4)
        return q * 4 + p if h == 0 else p * 4 + q

    barrier = pltpu.get_barrier_semaphore()

    @pl.loop(1, 16)
    def _(off):
        v = lax.rem(z + off // 4, 4) * 4 + lax.rem(x + off, 4)
        pl.semaphore_signal(barrier, inc=1, device_id={"vir": v}, device_id_type=MESH)

    @pl.loop(1, 8)
    def _(off):
        pl.semaphore_signal(barrier, inc=1, device_id={"occ": lax.rem(mine + off, 8)}, device_id_type=MESH)

    labs = lab_ref[...].reshape(1, nv)
    mylab = virs_ref[me * la]
    jocc = [occ_ref[2 * mine + j] for j in range(2)]

    quarter = lax.broadcasted_iota(jnp.int32, (la, nv), 1) // WIN

    def pack(h):
        both = []
        for kp in range(2):
            total = None
            for k2 in range(2):
                k = 4 * h + 2 * kp + k2
                for j in range(2):
                    want = kocc_ref[k] ^ jocc[j] ^ mylab
                    part = jnp.where(labs == want, w_ref[k, :, j, :].astype(jnp.float32), 0.0)
                    part = part + pltpu.roll(part, 2 * WIN, 1)
                    part = part + pltpu.roll(part, WIN, 1)
                    total = part if total is None else jnp.where(quarter >= 2 * k2 + j, part, total)
            both.append(total)
        panels[h, me] = jnp.concatenate(both, axis=0).astype(jnp.bfloat16)

    copies = []

    def send(h, block, rows, step, slot):
        p, q = here[h]
        ref = panels.at[h, at(h, p + block[0], q + block[1]), pl.ds(rows[0], rows[1] - rows[0])]
        c = pltpu.make_async_remote_copy(
            src_ref=ref, dst_ref=ref, send_sem=send_sem.at[h, slot], recv_sem=recv_sem.at[h, slot],
            device_id={"vir": at(h, p + step[0], q + step[1])}, device_id_type=MESH)
        c.start()
        copies.append(c)

    def arrived(h, block, rows, slot):
        p, q = here[h]
        ref = panels.at[h, at(h, p + block[0], q + block[1]), pl.ds(rows[0], rows[1] - rows[0])]
        pltpu.make_async_remote_copy(
            src_ref=ref, dst_ref=ref, send_sem=send_sem.at[h, slot], recv_sem=recv_sem.at[h, slot],
            device_id={"vir": me}, device_id_type=MESH).wait_recv()

    full = (0, 2 * la)

    def halves(h, turn):
        middle = 48 if (h + turn) % 2 else 32
        return (0, middle), (middle, 2 * la)


    def second(h, d):
        send(h, (d, 0), full, (0, 1), 4 + 4 * d)
        send(h, (d, 0), full, (0, -1), 5 + 4 * d)

    def relay(h, d):
        b = d if d < 2 else d - 4
        low, high = halves(h, d % 2)
        arrived(h, (b, -1), full, 4 + 4 * d)
        send(h, (b, -1), low, (0, 1), 6 + 4 * d)
        arrived(h, (b, 1), full, 5 + 4 * d)
        send(h, (b, 1), high, (0, -1), 7 + 4 * d)

    rows = la * nk

    def prepare(low, high):
        @pl.loop(low, high)
        def _(i):
            parts = []
            for s in range(2):
                orb = tab[ORDER + 2 * i + s]
                moved = jnp.dot(rowp[...], amp[orb].reshape(rows, nv), preferred_element_type=jnp.float32)
                left = occ_ref[orb] ^ mylab
                parts.append([
                    jnp.where(labs == (left ^ kocc_ref[k]), moved[k * la:(k + 1) * la], 0.0)
                    for k in range(nk)])
            here_rows = pl.ds(pl.multiple_of(2 * la * i, 16), 2 * la)
            for k in range(nk):
                tk[k, here_rows, :] = jnp.concatenate([parts[0][k], parts[1][k]], axis=0).astype(jnp.bfloat16)

    def multiply_row(dq, first):
        q = lax.rem(z + dq + 4, 4)
        blocks = [panels[0, 4 * q + p].astype(jnp.float32) for p in range(4)]
        for kp in range(2):
            row_wk[q, pl.ds(pl.multiple_of(256 * kp + 32 * q, 32), WIN), :] = jnp.concatenate(
                [b[kp * la:(kp + 1) * la] for b in blocks], axis=0).astype(jnp.bfloat16)
        lanes = pl.ds(pl.multiple_of(128 * q, 128), 256)
        for k2 in range(2):
            t = jnp.concatenate([tk[k2, :, lanes], tk[2 + k2, :, lanes]], axis=1)
            part = jnp.dot(t, row_wk[q, :, 256 * k2:256 * k2 + 384], preferred_element_type=jnp.float32)
            acc[k2] = part if first else acc[k2] + part

    def multiply_rest():
        for v in range(0, 16, 2):
            one, two = panels[1, v].astype(jnp.float32), panels[1, v + 1].astype(jnp.float32)
            for kp in range(2):
                wk[nv * kp + v * la:nv * kp + (v + 2) * la, :] = jnp.concatenate(
                    [one[kp * la:(kp + 1) * la], two[kp * la:(kp + 1) * la]], axis=0).astype(jnp.bfloat16)
        for k2 in range(2):
            t = jnp.concatenate([tk[4 + k2], tk[6 + k2]], axis=1)
            acc[k2] += jnp.dot(t, wk[:, 256 * k2:256 * k2 + 384], preferred_element_type=jnp.float32)

    pack(0)
    pl.semaphore_wait(barrier, 22)
    send(0, (0, 0), full, (1, 0), 0)
    send(0, (0, 0), full, (-1, 0), 1)
    second(0, 0)
    pack(1)
    send(1, (0, 0), full, (1, 0), 0)
    send(1, (0, 0), full, (-1, 0), 1)
    second(1, 0)
    r = lax.broadcasted_iota(jnp.int32, (rows, rows), 0)
    c = lax.broadcasted_iota(jnp.int32, (rows, rows), 1)
    rowp[...] = (c == lax.rem(r, la) * nk + r // la).astype(jnp.float32).astype(jnp.bfloat16)
    row_wk[...] = jnp.zeros(row_wk.shape, row_wk.dtype)
    for c in amp_copies:
        c.wait()
    prepare(0, 2)
    for h in range(2):
        low, high = halves(h, 0)
        arrived(h, (-1, 0), full, 0)
        send(h, (-1, 0), low, (1, 0), 2)
        second(h, 3)
        arrived(h, (1, 0), full, 1)
        send(h, (1, 0), high, (-1, 0), 3)
        second(h, 1)
    prepare(2, 3)
    for h in range(2):
        relay(h, 0)
    for h in range(2):
        low, high = halves(h, 0)
        arrived(h, (-2, 0), low, 2)
        arrived(h, (-2, 0), high, 3)
        second(h, 2)
    prepare(3, 5)
    for h in range(2):
        relay(h, 3)
    prepare(5, 6)
    for h in range(2):
        relay(h, 1)
    prepare(6, 8)
    for h in range(2):
        relay(h, 2)
    multiply_row(0, True)
    multiply_row(-1, False)
    multiply_row(1, False)

    def complete(h):
        for d in range(4):
            b = d if d < 2 else d - 4
            low, high = halves(h, d % 2)
            arrived(h, (b, 2), low, 6 + 4 * d)
            arrived(h, (b, 2), high, 7 + 4 * d)

    complete(0)
    multiply_row(2, False)
    complete(1)
    multiply_rest()

    whole = acc[0] + pltpu.roll(acc[1], 320, 1)
    wide = lax.broadcasted_iota(jnp.int32, whole.shape, 1)
    flatw = jnp.where(wide < 2 * WIN, whole, 0.0).astype(jnp.bfloat16).astype(jnp.float32)
    cw[...] = flatw.reshape(batch, la, 384)

    spot = lax.broadcasted_iota(jnp.int32, (batch * la, 128), 1)
    for j in range(2):
        for r in range(4):
            start = WIN * j + la * r
            tile = start // 128 * 128
            width = 128 if start + la <= tile + 128 else 256
            total = None
            for g in range(3):
                piece = flatw[g * la:, tile:tile + width]
                shift = (la * g - (start - tile)) % width
                if shift:
                    piece = pltpu.roll(piece, shift, 1)
                piece = piece[:, :128]
                if g:
                    piece = jnp.concatenate([piece, jnp.zeros((g * la, 128), jnp.float32)], axis=0)
                total = piece if g == 0 else jnp.where(spot >= g * la, piece, total)
            comb[4 * j + r] = total.reshape(batch, la, 128)

    def message(r, v):
        lab = virs_ref[v * la]
        parts = []
        for j in range(2):
            base = tab[BEGIN + (jocc[j] ^ lab ^ mylab)]
            for q in range(groups):
                parts.append(comb[4 * j + r, base + 3 * q])
        return jnp.concatenate(parts, axis=0).astype(jnp.bfloat16)

    def far_copy(off, v, source):
        return pltpu.make_async_remote_copy(
            src_ref=far.at[v], dst_ref=near.at[source], send_sem=far_send.at[off], recv_sem=far_recv.at[off],
            device_id={"vir": v}, device_id_type=MESH)

    offs = [10, 9, 11, 6, 14, 2, 8, 5, 7, 13, 15, 1, 3, 4, 12]
    for off in offs:
        v = at(0, x + off % 4, z + off // 4)
        far[v] = message(lax.rem(x + off % 4, 4), v)
        far_copy(off, v, me).start()
    near[me] = message(x, me)
    nearf[me] = near[me].astype(jnp.float32).reshape(2 * groups, la, 128)
    for off in reversed(offs):
        source = at(0, x - off % 4, z - off // 4)
        pltpu.make_async_remote_copy(
            src_ref=near.at[source], dst_ref=near.at[source], send_sem=far_send.at[off], recv_sem=far_recv.at[off],
            device_id={"vir": source}, device_id_type=MESH).wait_recv()
        nearf[source] = near[source].astype(jnp.float32).reshape(2 * groups, la, 128)

    def windows(o):
        both = []
        for j in range(2):
            wins = []
            for s in range(2):
                orb = 2 * o + s
                lab = occ_ref[orb]
                want = lab ^ mylab ^ jocc[j]
                row = groups * j + tab[GROUP + orb]
                stack = [nearf[tab[BLOCK + 4 * want + d], row] for d in range(4)]
                stack = jnp.concatenate(stack + [jnp.zeros((96, 128), jnp.float32)], axis=0).T
                for m in range(3):
                    turned[2 * j + s, m] = stack[m * la:(m + 1) * la]
                win = turned[2 * j + s, tab[MEMBER + orb]]
                wins.append(jnp.concatenate([win, jnp.zeros((la, 128), jnp.float32)], axis=1))
            both.append(wins[0] + pltpu.roll(wins[1], WIN, 1))
        return jnp.concatenate(both, axis=0).astype(jnp.bfloat16)

    def occ_copy(off, o, source):
        return pltpu.make_async_remote_copy(
            src_ref=pack_out.at[o], dst_ref=pack_in.at[source], send_sem=occ_send.at[off], recv_sem=occ_recv.at[off],
            device_id={"occ": o}, device_id_type=MESH)

    order_occ = [4, 5, 3, 2, 6, 7, 1]
    for off in order_occ:
        o = lax.rem(mine + off, 8)
        pack_out[o] = windows(o)
        occ_copy(off, o, mine).start()
    pack_in[mine] = windows(mine)

    tile_no = lax.broadcasted_iota(jnp.int32, (la, 640), 1) // WIN
    even = lax.rem(tile_no, 2) == 0

    def finish(o):
        back = pack_in[o].astype(jnp.float32)
        for j2 in range(2):
            orb = 2 * o + j2
            own_rows = cw[tab[PLACE + orb]]
            both = own_rows + back[j2 * la:(j2 + 1) * la]
            both = jnp.concatenate([both, jnp.zeros((la, 256), jnp.float32)], axis=1)
            both = both + pltpu.roll(both, 2 * WIN, 1)
            turn = pltpu.roll(both, WIN, 1)
            for j in range(2):
                want = occ_ref[orb] ^ mylab ^ jocc[j]
                row = jnp.where(even, both, turn) if j == 0 else jnp.where(even, turn, both)
                out_ref[orb, j] = jnp.where(labs == want, row, 0.0).astype(jnp.bfloat16)

    finish(mine)
    for off in reversed(order_occ):
        source = lax.rem(mine + 8 - off, 8)
        pltpu.make_async_remote_copy(
            src_ref=pack_in.at[source], dst_ref=pack_in.at[source], send_sem=occ_send.at[off],
            recv_sem=occ_recv.at[off], device_id={"occ": source}, device_id_type=MESH).wait_recv()
        finish(source)
    for c in copies:
        c.wait_send()
    for off in offs:
        far_copy(off, at(0, x + off % 4, z + off // 4), me).wait_send()
    for off in order_occ:
        occ_copy(off, lax.rem(mine + off, 8), mine).wait_send()


def residual_rows(groups, collective, amplitude, integral, occ_irrep, kocc_irrep, vir_irrep, table):
    batch, la, nk, nv = amplitude.shape
    rows = 2 * groups * la
    smem, vmem = pl.BlockSpec(memory_space=pltpu.SMEM), pl.BlockSpec(memory_space=pltpu.VMEM)
    return pl.pallas_call(
        functools.partial(cycle_kernel, groups),
        out_shape=jax.ShapeDtypeStruct((batch, 2, la, nv), jnp.bfloat16),
        in_specs=[pl.BlockSpec(memory_space=pl.ANY), vmem, smem, smem, vmem, smem, smem],
        out_specs=vmem,
        scratch_shapes=[
            pltpu.VMEM((batch, la, nk, nv), jnp.bfloat16),
            pltpu.VMEM((2, 16, 2 * la, 640), jnp.bfloat16),
            pltpu.VMEM((nk, batch * la, nv), jnp.bfloat16),
            pltpu.VMEM((4, 512, 640), jnp.bfloat16),
            pltpu.VMEM((2 * nv, 640), jnp.bfloat16),
            pltpu.VMEM((2, batch * la, 384), jnp.float32),
            pltpu.VMEM((la * nk, la * nk), jnp.bfloat16),
            pltpu.VMEM((batch, la, 384), jnp.float32),
            pltpu.VMEM((8, batch, la, 128), jnp.float32),
            pltpu.VMEM((16, rows, 128), jnp.bfloat16),
            pltpu.VMEM((16, rows, 128), jnp.bfloat16),
            pltpu.VMEM((16, 2 * groups, la, 128), jnp.float32),
            pltpu.VMEM((4, 3, la, 256), jnp.float32),
            pltpu.VMEM((8, 2 * la, 384), jnp.bfloat16),
            pltpu.VMEM((8, 2 * la, 384), jnp.bfloat16),
            pltpu.SemaphoreType.DMA((batch // 2,)),
            pltpu.SemaphoreType.DMA((2, 20)),
            pltpu.SemaphoreType.DMA((2, 20)),
            pltpu.SemaphoreType.DMA((16,)),
            pltpu.SemaphoreType.DMA((16,)),
            pltpu.SemaphoreType.DMA((8,)),
            pltpu.SemaphoreType.DMA((8,)),
        ],
        compiler_params=pltpu.CompilerParams(
            collective_id=collective, has_side_effects=True, vmem_limit_bytes=56 * 1024 * 1024),
        name="cycle_residual",
    )(amplitude, integral, occ_irrep, kocc_irrep, vir_irrep, vir_irrep, table)


def shards(amplitude, integral, occ_irrep, kocc_irrep, vir_irrep):
    table = make_table(2, occ_irrep, vir_irrep)
    args = (amplitude, integral, occ_irrep, kocc_irrep, vir_irrep)
    rows = lax.cond(
        table[MOST] <= FEW,
        lambda *a: residual_rows(2, 0, *a, table),
        lambda *a: residual_rows(6, 1, *a, make_table(6, occ_irrep, vir_irrep)),
        *args,
    )
    return jnp.transpose(rows, (0, 2, 1, 3))


def solution(mesh):
    in_specs = (P(None, "vir", None, None), P(None, "vir", "occ", None), P(), P(), P())
    out_specs = P(None, "vir", "occ", None)
    return jax.shard_map(shards, mesh=mesh, in_specs=in_specs, out_specs=out_specs, check_vma=False)
```

```python
import functools
import jax
import jax.numpy as jnp
from jax import lax
from jax.experimental import pallas as pl
from jax.experimental.pallas import tpu as pltpu
from jax.sharding import PartitionSpec as P

WIN = 160
FEW = 6
MESH = pl.DeviceIdType.MESH
ORDER, PLACE, BEGIN, BLOCK, GROUP, MEMBER, MOST = 0, 16, 32, 40, 72, 88, 104


def table_kernel(groups, occ_ref, virs_ref, tab):
    batch = occ_ref.shape[0]
    la = virs_ref.shape[0] // 16
    occ = [occ_ref[i] for i in range(batch)]
    places = [jnp.int32(0)] * batch
    for i in range(batch):
        for o in range(i):
            before = (occ[o] <= occ[i]).astype(jnp.int32)
            places[i] = places[i] + before
            places[o] = places[o] + (1 - before)
    below = []
    for r in range(8):
        total = jnp.int32(0)
        for o in range(batch):
            total = total + (occ[o] < r).astype(jnp.int32)
        below.append(total)
    below.append(jnp.int32(batch))
    most = jnp.int32(0)
    for r in range(8):
        most = jnp.maximum(most, below[r + 1] - below[r])
        tab[BEGIN + r] = jnp.minimum(below[r], max(batch - 3 * groups, 0))
        for d in range(4):
            tab[BLOCK + 4 * r + d] = jnp.int32(0)
    tab[MOST] = most
    for v in range(16):
        tab[BLOCK + 4 * virs_ref[la * v] + v % 4] = jnp.int32(v)
    for i in range(batch):
        tab[PLACE + i] = places[i]
        tab[ORDER + places[i]] = jnp.int32(i)
        slot = places[i] - tab[BEGIN + occ[i]]
        group = jnp.int32(0)
        for q in range(1, groups):
            group = group + (slot >= 3 * q).astype(jnp.int32)
        tab[GROUP + i] = group
        tab[MEMBER + i] = slot - 3 * group


def make_table(groups, occ_irrep, vir_irrep):
    smem = pl.BlockSpec(memory_space=pltpu.SMEM)
    return pl.pallas_call(
        functools.partial(table_kernel, groups),
        out_shape=jax.ShapeDtypeStruct((105,), jnp.int32),
        in_specs=[smem, smem],
        out_specs=smem,
        name="make_table",
    )(occ_irrep, vir_irrep)


def cycle_kernel(groups, amp_ref, w_ref, occ_ref, kocc_ref, lab_ref, virs_ref, tab, out_ref,
                 amp, panels, tk, row_wk, wk, acc, rowp, cw, comb, far, near, nearf, turned, pack_out, pack_in,
                 amp_sem, send_sem, recv_sem, far_send, far_recv, occ_send, occ_recv):
    me = lax.axis_index("vir")
    mine = lax.axis_index("occ")
    z, x = me // 4, lax.rem(me, 4)
    batch, la, nk, nv = amp.shape
    pairs = batch // 2
    here = [(x, z), (z, x)]

    amp_copies = [
        pltpu.make_async_copy(amp_ref.at[pl.ds(2 * i, 2)], amp.at[pl.ds(2 * i, 2)], amp_sem.at[i])
        for i in range(pairs)]
    for c in amp_copies:
        c.start()

    def at(h, p, q):
        p, q = lax.rem(p + 8, 4), lax.rem(q + 8, 4)
        return q * 4 + p if h == 0 else p * 4 + q

    barrier = pltpu.get_barrier_semaphore()

    @pl.loop(1, 16)
    def _(off):
        v = lax.rem(z + off // 4, 4) * 4 + lax.rem(x + off, 4)
        pl.semaphore_signal(barrier, inc=1, device_id={"vir": v}, device_id_type=MESH)

    @pl.loop(1, 8)
    def _(off):
        pl.semaphore_signal(barrier, inc=1, device_id={"occ": lax.rem(mine + off, 8)}, device_id_type=MESH)

    labs = lab_ref[...].reshape(1, nv)
    mylab = virs_ref[me * la]
    jocc = [occ_ref[2 * mine + j] for j in range(2)]

    quarter = lax.broadcasted_iota(jnp.int32, (la, nv), 1) // WIN

    def pack(h):
        both = []
        for kp in range(2):
            total = None
            for k2 in range(2):
                k = 4 * h + 2 * kp + k2
                for j in range(2):
                    want = kocc_ref[k] ^ jocc[j] ^ mylab
                    part = jnp.where(labs == want, w_ref[k, :, j, :].astype(jnp.float32), 0.0)
                    part = part + pltpu.roll(part, 2 * WIN, 1)
                    part = part + pltpu.roll(part, WIN, 1)
                    total = part if total is None else jnp.where(quarter >= 2 * k2 + j, part, total)
            both.append(total)
        panels[h, me] = jnp.concatenate(both, axis=0).astype(jnp.bfloat16)

    copies = []

    def send(h, block, rows, step, slot):
        p, q = here[h]
        ref = panels.at[h, at(h, p + block[0], q + block[1]), pl.ds(rows[0], rows[1] - rows[0])]
        c = pltpu.make_async_remote_copy(
            src_ref=ref, dst_ref=ref, send_sem=send_sem.at[h, slot], recv_sem=recv_sem.at[h, slot],
            device_id={"vir": at(h, p + step[0], q + step[1])}, device_id_type=MESH)
        c.start()
        copies.append(c)

    def arrived(h, block, rows, slot):
        p, q = here[h]
        ref = panels.at[h, at(h, p + block[0], q + block[1]), pl.ds(rows[0], rows[1] - rows[0])]
        pltpu.make_async_remote_copy(
            src_ref=ref, dst_ref=ref, send_sem=send_sem.at[h, slot], recv_sem=recv_sem.at[h, slot],
            device_id={"vir": me}, device_id_type=MESH).wait_recv()

    full = (0, 2 * la)

    def halves(h, turn):
        middle = 48 if (h + turn) % 2 else 32
        return (0, middle), (middle, 2 * la)


    def second(h, d):
        send(h, (d, 0), full, (0, 1), 4 + 4 * d)
        send(h, (d, 0), full, (0, -1), 5 + 4 * d)

    def relay(h, d):
        b = d if d < 2 else d - 4
        low, high = halves(h, d % 2)
        arrived(h, (b, -1), full, 4 + 4 * d)
        send(h, (b, -1), low, (0, 1), 6 + 4 * d)
        arrived(h, (b, 1), full, 5 + 4 * d)
        send(h, (b, 1), high, (0, -1), 7 + 4 * d)

    rows = la * nk

    def prepare(low, high):
        @pl.loop(low, high)
        def _(i):
            parts = []
            for s in range(2):
                orb = tab[ORDER + 2 * i + s]
                moved = jnp.dot(rowp[...], amp[orb].reshape(rows, nv), preferred_element_type=jnp.float32)
                left = occ_ref[orb] ^ mylab
                parts.append([
                    jnp.where(labs == (left ^ kocc_ref[k]), moved[k * la:(k + 1) * la], 0.0)
                    for k in range(nk)])
            here_rows = pl.ds(pl.multiple_of(2 * la * i, 16), 2 * la)
            for k in range(nk):
                tk[k, here_rows, :] = jnp.concatenate([parts[0][k], parts[1][k]], axis=0).astype(jnp.bfloat16)

    def multiply_row(dq, first):
        q = lax.rem(z + dq + 4, 4)
        blocks = [panels[0, 4 * q + p].astype(jnp.float32) for p in range(4)]
        for kp in range(2):
            row_wk[q, pl.ds(pl.multiple_of(256 * kp + 32 * q, 32), WIN), :] = jnp.concatenate(
                [b[kp * la:(kp + 1) * la] for b in blocks], axis=0).astype(jnp.bfloat16)
        lanes = pl.ds(pl.multiple_of(128 * q, 128), 256)
        for k2 in range(2):
            t = jnp.concatenate([tk[k2, :, lanes], tk[2 + k2, :, lanes]], axis=1)
            part = jnp.dot(t, row_wk[q, :, 256 * k2:256 * k2 + 384], preferred_element_type=jnp.float32)
            acc[k2] = part if first else acc[k2] + part

    def order_rows(half):
        for zz in range(4):
            v = 4 * zz + 2 * half
            one, two = panels[1, v].astype(jnp.float32), panels[1, v + 1].astype(jnp.float32)
            for kp in range(2):
                wk[pl.ds(pl.multiple_of(nv * kp + v * la, 16), 2 * la), :] = jnp.concatenate(
                    [one[kp * la:(kp + 1) * la], two[kp * la:(kp + 1) * la]], axis=0).astype(jnp.bfloat16)

    def multiply_rest():
        for k2 in range(2):
            t = jnp.concatenate([tk[4 + k2], tk[6 + k2]], axis=1)
            acc[k2] += jnp.dot(t, wk[:, 256 * k2:256 * k2 + 384], preferred_element_type=jnp.float32)

    pack(0)
    pl.semaphore_wait(barrier, 22)
    send(0, (0, 0), full, (1, 0), 0)
    send(0, (0, 0), full, (-1, 0), 1)
    second(0, 0)
    pack(1)
    send(1, (0, 0), full, (1, 0), 0)
    send(1, (0, 0), full, (-1, 0), 1)
    second(1, 0)
    r = lax.broadcasted_iota(jnp.int32, (rows, rows), 0)
    c = lax.broadcasted_iota(jnp.int32, (rows, rows), 1)
    rowp[...] = (c == lax.rem(r, la) * nk + r // la).astype(jnp.float32).astype(jnp.bfloat16)
    row_wk[...] = jnp.zeros(row_wk.shape, row_wk.dtype)
    for c in amp_copies:
        c.wait()
    prepare(0, 2)
    for h in range(2):
        low, high = halves(h, 0)
        arrived(h, (-1, 0), full, 0)
        send(h, (-1, 0), low, (1, 0), 2)
        second(h, 3)
        arrived(h, (1, 0), full, 1)
        send(h, (1, 0), high, (-1, 0), 3)
        second(h, 1)
    prepare(2, 3)
    for h in range(2):
        relay(h, 0)
    for h in range(2):
        low, high = halves(h, 0)
        arrived(h, (-2, 0), low, 2)
        arrived(h, (-2, 0), high, 3)
        second(h, 2)
    prepare(3, 5)
    for h in range(2):
        relay(h, 3)
    prepare(5, 6)
    for h in range(2):
        relay(h, 1)
    prepare(6, 8)
    for h in range(2):
        relay(h, 2)
    order_rows(x // 2)
    multiply_row(0, True)
    multiply_row(-1, False)
    multiply_row(1, False)

    def complete(h):
        for d in range(4):
            b = d if d < 2 else d - 4
            low, high = halves(h, d % 2)
            arrived(h, (b, 2), low, 6 + 4 * d)
            arrived(h, (b, 2), high, 7 + 4 * d)

    complete(0)
    multiply_row(2, False)
    complete(1)
    order_rows(1 - x // 2)
    multiply_rest()

    whole = acc[0] + pltpu.roll(acc[1], 320, 1)
    wide = lax.broadcasted_iota(jnp.int32, whole.shape, 1)
    flatw = jnp.where(wide < 2 * WIN, whole, 0.0).astype(jnp.bfloat16).astype(jnp.float32)
    cw[...] = flatw.reshape(batch, la, 384)

    spot = lax.broadcasted_iota(jnp.int32, (batch * la, 128), 1)
    def combine(j, r):
        start = WIN * j + la * r
        tile = start // 128 * 128
        width = 128 if start + la <= tile + 128 else 256
        total = None
        for g in range(3):
            piece = flatw[g * la:, tile:tile + width]
            shift = (la * g - (start - tile)) % width
            if shift:
                piece = pltpu.roll(piece, shift, 1)
            piece = piece[:, :128]
            if g:
                piece = jnp.concatenate([piece, jnp.zeros((g * la, 128), jnp.float32)], axis=0)
            total = piece if g == 0 else jnp.where(spot >= g * la, piece, total)
        comb[4 * j + r] = total.reshape(batch, la, 128)

    def message(r, v):
        lab = virs_ref[v * la]
        parts = []
        for j in range(2):
            base = tab[BEGIN + (jocc[j] ^ lab ^ mylab)]
            for q in range(groups):
                parts.append(comb[4 * j + r, base + 3 * q])
        return jnp.concatenate(parts, axis=0).astype(jnp.bfloat16)

    def far_copy(off, v, source):
        return pltpu.make_async_remote_copy(
            src_ref=far.at[v], dst_ref=near.at[source], send_sem=far_send.at[off], recv_sem=far_recv.at[off],
            device_id={"vir": v}, device_id_type=MESH)

    def each(offsets, body):
        if groups == 2:
            for off in offsets:
                body(off)
        else:
            pl.loop(1, len(offsets) + 1)(body)

    def beside(off):
        off = jnp.int32(off)
        return lax.rem(z + off // 4, 4) * 4 + lax.rem(x + off, 4)

    def behind(off):
        off = jnp.int32(off)
        return lax.rem(z + 4 - off // 4, 4) * 4 + lax.rem(x + 16 - off, 4)

    offs = [10, 9, 11, 6, 14, 2, 8, 5, 7, 13, 15, 1, 3, 4, 12]

    for r in range(4):
        for j in range(2):
            combine(j, r)
        for dz in (2, 1, 3, 0):
            v = lax.rem(z + dz, 4) * 4 + r
            off = 4 * dz + lax.rem(r + 4 - x, 4)
            far[v] = message(r, v)
            if dz:
                far_copy(off, v, me).start()
            else:
                @pl.when(off != 0)
                def _():
                    far_copy(off, v, me).start()
    near[me] = far[me]
    nearf[me] = near[me].astype(jnp.float32).reshape(2 * groups, la, 128)

    def take_far(off):
        source = behind(off)
        pltpu.make_async_remote_copy(
            src_ref=near.at[source], dst_ref=near.at[source], send_sem=far_send.at[off], recv_sem=far_recv.at[off],
            device_id={"vir": source}, device_id_type=MESH).wait_recv()
        nearf[source] = near[source].astype(jnp.float32).reshape(2 * groups, la, 128)

    each(offs[::-1], take_far)

    def windows(o):
        both = []
        for j in range(2):
            wins = []
            for s in range(2):
                orb = 2 * o + s
                lab = occ_ref[orb]
                want = lab ^ mylab ^ jocc[j]
                row = groups * j + tab[GROUP + orb]
                stack = [nearf[tab[BLOCK + 4 * want + d], row] for d in range(4)]
                stack = jnp.concatenate(stack + [jnp.zeros((96, 128), jnp.float32)], axis=0).T
                for m in range(3):
                    turned[2 * j + s, m] = stack[m * la:(m + 1) * la]
                win = turned[2 * j + s, tab[MEMBER + orb]]
                wins.append(jnp.concatenate([win, jnp.zeros((la, 128), jnp.float32)], axis=1))
            both.append(wins[0] + pltpu.roll(wins[1], WIN, 1))
        rest = both[0][:, 256:] + pltpu.roll(both[1][:, 256:], 64, 1)
        return jnp.concatenate(
            [both[0][:, :128], both[1][:, :128], both[0][:, 128:256], both[1][:, 128:256], rest,
             jnp.zeros((8, 128), jnp.float32)], axis=0).astype(jnp.bfloat16)

    def occ_copy(off, o, source):
        return pltpu.make_async_remote_copy(
            src_ref=pack_out.at[o], dst_ref=pack_in.at[source], send_sem=occ_send.at[off], recv_sem=occ_recv.at[off],
            device_id={"occ": o}, device_id_type=MESH)

    order_occ = [4, 5, 3, 2, 6, 7, 1]

    def send_occ(off):
        o = lax.rem(mine + off, 8)
        pack_out[o] = windows(o)
        occ_copy(off, o, mine).start()

    each(order_occ, send_occ)
    pack_in[mine] = windows(mine)

    tile_no = lax.broadcasted_iota(jnp.int32, (la, 640), 1) // WIN
    even = lax.rem(tile_no, 2) == 0

    thin = lax.broadcasted_iota(jnp.int32, (la, 128), 1) < 64

    def finish(o):
        back = pack_in[o].astype(jnp.float32)
        rest = back[4 * la:5 * la]
        for j2 in range(2):
            orb = 2 * o + j2
            if j2:
                rest = pltpu.roll(rest, 64, 1)
            both = cw[tab[PLACE + orb]] + jnp.concatenate(
                [back[j2 * la:(j2 + 1) * la], back[(2 + j2) * la:(3 + j2) * la], jnp.where(thin, rest, 0.0)], axis=1)
            both = jnp.concatenate([both, jnp.zeros((la, 256), jnp.float32)], axis=1)
            both = both + pltpu.roll(both, 2 * WIN, 1)
            turn = pltpu.roll(both, WIN, 1)
            for j in range(2):
                want = occ_ref[orb] ^ mylab ^ jocc[j]
                row = jnp.where(even, both, turn) if j == 0 else jnp.where(even, turn, both)
                out_ref[orb, j] = jnp.where(labs == want, row, 0.0).astype(jnp.bfloat16)

    finish(mine)

    def take_occ(off):
        source = lax.rem(mine + 8 - off, 8)
        pltpu.make_async_remote_copy(
            src_ref=pack_in.at[source], dst_ref=pack_in.at[source], send_sem=occ_send.at[off],
            recv_sem=occ_recv.at[off], device_id={"occ": source}, device_id_type=MESH).wait_recv()
        finish(source)

    each(order_occ[::-1], take_occ)
    for c in copies:
        c.wait_send()
    each(offs, lambda off: far_copy(off, beside(off), me).wait_send())
    each(order_occ, lambda off: occ_copy(off, lax.rem(mine + off, 8), mine).wait_send())


def residual_rows(groups, collective, amplitude, integral, occ_irrep, kocc_irrep, vir_irrep, table):
    batch, la, nk, nv = amplitude.shape
    rows = 2 * groups * la
    smem, vmem = pl.BlockSpec(memory_space=pltpu.SMEM), pl.BlockSpec(memory_space=pltpu.VMEM)
    return pl.pallas_call(
        functools.partial(cycle_kernel, groups),
        out_shape=jax.ShapeDtypeStruct((batch, 2, la, nv), jnp.bfloat16),
        in_specs=[pl.BlockSpec(memory_space=pl.ANY), vmem, smem, smem, vmem, smem, smem],
        out_specs=vmem,
        scratch_shapes=[
            pltpu.VMEM((batch, la, nk, nv), jnp.bfloat16),
            pltpu.VMEM((2, 16, 2 * la, 640), jnp.bfloat16),
            pltpu.VMEM((nk, batch * la, nv), jnp.bfloat16),
            pltpu.VMEM((4, 512, 640), jnp.bfloat16),
            pltpu.VMEM((2 * nv, 640), jnp.bfloat16),
            pltpu.VMEM((2, batch * la, 384), jnp.float32),
            pltpu.VMEM((la * nk, la * nk), jnp.bfloat16),
            pltpu.VMEM((batch, la, 384), jnp.float32),
            pltpu.VMEM((8, batch, la, 128), jnp.float32),
            pltpu.VMEM((16, rows, 128), jnp.bfloat16),
            pltpu.VMEM((16, rows, 128), jnp.bfloat16),
            pltpu.VMEM((16, 2 * groups, la, 128), jnp.float32),
            pltpu.VMEM((4, 3, la, 256), jnp.float32),
            pltpu.VMEM((8, 208, 128), jnp.bfloat16),
            pltpu.VMEM((8, 208, 128), jnp.bfloat16),
            pltpu.SemaphoreType.DMA((batch // 2,)),
            pltpu.SemaphoreType.DMA((2, 20)),
            pltpu.SemaphoreType.DMA((2, 20)),
            pltpu.SemaphoreType.DMA((16,)),
            pltpu.SemaphoreType.DMA((16,)),
            pltpu.SemaphoreType.DMA((8,)),
            pltpu.SemaphoreType.DMA((8,)),
        ],
        compiler_params=pltpu.CompilerParams(
            collective_id=collective, has_side_effects=True, vmem_limit_bytes=56 * 1024 * 1024),
        name="cycle_residual",
    )(amplitude, integral, occ_irrep, kocc_irrep, vir_irrep, vir_irrep, table)


def shards(amplitude, integral, occ_irrep, kocc_irrep, vir_irrep):
    table = make_table(2, occ_irrep, vir_irrep)
    args = (amplitude, integral, occ_irrep, kocc_irrep, vir_irrep)
    rows = lax.cond(
        table[MOST] <= FEW,
        lambda *a: residual_rows(2, 0, *a, table),
        lambda *a: residual_rows(6, 1, *a, make_table(6, occ_irrep, vir_irrep)),
        *args,
    )
    return jnp.transpose(rows, (0, 2, 1, 3))


def solution(mesh):
    in_specs = (P(None, "vir", None, None), P(None, "vir", "occ", None), P(), P(), P())
    out_specs = P(None, "vir", "occ", None)
    return jax.shard_map(shards, mesh=mesh, in_specs=in_specs, out_specs=out_specs, check_vma=False)
```
